32 devices in a mesh: ent: 8 (over y, x, core), rel: 4 (over z).
Axes of the slice: x: 2, y: 2, z: 4, core: 2. Of those that a mesh axis runs over, the one named last changes fastest.
Arguments:
- entity_table: bfloat16 [128, 1024], P('ent'), may hold values from -1.5 to 1.5
- phases: float32 [4096, 512], P('rel'), may hold values from -3.140625 to 3.140625
- head_owner: int32 [16384, 1], P(('ent', 'rel')), may hold values from 0 to 31; in each aligned block of 512 rows (0 to 511, 512 to 1023, ...) at most 32 rows name the same one
- head_row: int32 [16384], P(('ent', 'rel')), may hold values from 0 to 3
- relation: int32 [16384], P(('ent', 'rel')), may hold values from 0 to 1023
- tail_ids: int32 [16384], P(('ent', 'rel')), may hold values from 0 to 127
- known_tails: int32 [16384, 32], P(('ent', 'rel')), may hold values from 0 to 127
Outputs:
- entity_gradient: float32 [128, 1024], P(('ent', 'rel'))
- relation_gradient: float32 [4096, 512], P('rel')
The draws below stay inside these ranges and needn't reach their ends.
Inputs may be any that keep to these rules, and one draw needn't show every extreme that they name: `head_owner`: owner o of the 32 holds working-set rows o * 4 to o * 4 + 3 and is device (o // 4, o mod 4) of ent and rel. Among the 512 triples of one device at most 32 have heads held by one owner, and exactly 32 in some devices. The triples of block b of 512 belong to relation group b mod 4.
All inputs are finite; a program needn't handle non-finite values.
Results may differ from the reference program's by a relative error of at most 0.004.
Values may be sent and summed in bfloat16 or wider, within the bound.
No kernel may reach another device: no remote copies, remote signals or barrier semaphores. Data moves between devices by JAX's collectives and lax.ppermute only.
A program may use at most 64 MiB of HBM per device.

```python
import math
import jax
import jax.numpy as jnp
import numpy as np
from jax import lax

DIM = 512
WIDTH = 1024
RELS = 4096
LISTED = 32
TRIP_DEV = 512
OWNERS = 32
ENTITIES = 128
TRIPLES = 16384
REL_GRP = 1024
ROWS_OWN = 4
CAP = 32
N_REL = 4


def draw_entity_table(key, part):
    key_base, key_scale = jax.random.split(jax.random.fold_in(key, 11), 2)
    spread = jnp.exp(jax.random.uniform(key_scale, (ENTITIES, 1), jnp.float32, 0.0, math.log(1.5)))
    base = jnp.clip(jax.random.normal(key_base, (ENTITIES, WIDTH), jnp.float32), -5.0, 5.0)
    return (0.045 * base * spread).astype(jnp.bfloat16)


def plant(entries, own_key, smallest, top_value):
    longest = entries.shape.index(max(entries.shape))
    spots = []
    for shift in (0, 1):
        where = [jax.random.randint(jax.random.fold_in(own_key, axis), (), 0, length) for axis, length in enumerate(entries.shape)]
        where[longest] = (where[longest] + shift) % entries.shape[longest]
        spots.append(tuple(where))
    return entries.at[spots[0]].set(smallest).at[spots[1]].set(top_value)


def rank_bounds(amount, skew):
    loads = [(1 << 20) // math.isqrt(grade ** skew) + 1 for grade in range(1, amount + 1)]
    width = 1 + sum(loads) // (1 << 30)
    return np.cumsum(np.array([max(1, weight // width) for weight in loads]))


def ranked_ids(own_key, dims, count, slope):
    table = rank_bounds(count, slope)
    lot = jax.random.randint(jax.random.fold_in(own_key, 1), dims, 0, int(table[count - 1]))
    rank = jnp.searchsorted(jnp.asarray(table, jnp.int32), lot, side="right")
    return jax.random.permutation(jax.random.fold_in(own_key, 2), count)[rank].astype(jnp.int32)


def routed_block(key, own, number, rows, count, top, limit, lean):
    ranking = jax.random.permutation(key, count)
    crowded, usual = portions_of(count, rows * top, limit, lean, True), portions_of(count, rows * top, limit, lean, False)
    places = jnp.arange(count)

    def named(tallies, rotation):
        used = int((tallies > 0).sum())
        fixed = max(1, used // 4)
        shifted = fixed + (places - fixed + rotation * (used - fixed)) % max(1, count - fixed)
        return jnp.zeros((count,), jnp.int32).at[ranking[jnp.where(places < fixed, places, shifted)]].set(jnp.asarray(tallies, jnp.int32))

    tallies = jnp.where(number % 4 == 0, named(crowded, number // 4), named(usual, number - number // 4 - 1))
    mixed = jax.random.permutation(jax.random.fold_in(own, 3), count)
    giver, sink = mixed[0:count // 2 * 2:2], mixed[1:count // 2 * 2:2]
    room = jnp.minimum(tallies[giver] - 1, limit - tallies[sink]) // 2
    room = jnp.where((giver == ranking[0]) | (sink == ranking[0]) | (tallies[sink] == 0), 0, jnp.maximum(room, 0))
    shifted = jax.random.randint(jax.random.fold_in(own, 4), (count // 2,), 0, 1 << 20) % (room + 1)
    tallies = tallies.at[giver].add(-shifted).at[sink].add(shifted)
    labels = jnp.searchsorted(jnp.cumsum(tallies), jnp.arange(rows * top), side="right").astype(jnp.int32)
    listing = labels.reshape(top, rows).T
    listing = listing[jax.random.permutation(jax.random.fold_in(own, 1), rows)]
    rotation = jax.random.randint(jax.random.fold_in(own, 2), (rows, 1), 0, top)
    return jnp.take_along_axis(listing, (jnp.arange(top)[None, :] + rotation) % top, axis=1)


def portions_of(number_of, total, limit, slope, full):
    loads = [(1 << 20) // math.isqrt(grade ** slope) + 1 for grade in range(1, number_of + 1)]
    largest = limit if full else min(limit, max(-(-total // number_of), total * loads[0] // sum(loads)))
    least = 1 if total - largest >= number_of - 1 else 0
    given, surplus = [largest] + [least] * (number_of - 1), total - largest - least * (number_of - 1)
    while surplus > 0:
        candidates = [i for i in range(1, number_of) if given[i] < largest] or [i for i in range(1, number_of) if given[i] < limit]
        whole, left = sum([loads[i] for i in candidates]), surplus
        for i in candidates:
            extra = min(limit - given[i], max(1, left * loads[i] // whole), surplus)
            given[i] = given[i] + extra
            surplus = surplus - extra
    return np.array(given)


def setup_inputs(seed: int = 0) -> dict:
    key_of = jax.random.split(jax.random.key(seed), 8)
    entity_table = draw_entity_table(jax.random.fold_in(key_of[7], 71), 0)
    phases = jnp.clip(jax.random.uniform(key_of[1], (RELS, DIM), jnp.float32, -3.140625, 3.140625), -3.140625, 3.140625)
    head_owner_keys = jax.random.split(jax.random.fold_in(key_of[2], 1), TRIPLES // TRIP_DEV)
    head_owner_turns = jax.random.permutation(jax.random.fold_in(key_of[2], 3), TRIPLES // TRIP_DEV)
    head_owner = jax.vmap(lambda own, number: routed_block(jax.random.fold_in(key_of[2], 2), own, number, TRIP_DEV, OWNERS, 1, CAP, 2))(head_owner_keys, head_owner_turns).reshape((TRIPLES, 1))
    head_row = plant(ranked_ids(key_of[3], (TRIPLES,), ROWS_OWN, 2), jax.random.fold_in(key_of[3], 3), 0, ROWS_OWN - 1).astype(jnp.int32)
    relation = plant(jax.random.randint(key_of[4], (TRIPLES,), 0, REL_GRP), jax.random.fold_in(key_of[4], 1), 0, REL_GRP - 1).astype(jnp.int32)
    tail_ids = plant(jax.random.randint(key_of[5], (TRIPLES,), 0, ENTITIES), jax.random.fold_in(key_of[5], 1), 0, ENTITIES - 1).astype(jnp.int32)
    known_tails = plant(jax.random.randint(key_of[6], (TRIPLES, LISTED), 0, ENTITIES), jax.random.fold_in(key_of[6], 1), 0, ENTITIES - 1).astype(jnp.int32)
    return {"entity_table": entity_table, "phases": phases, "head_owner": head_owner, "head_row": head_row, "relation": relation, "tail_ids": tail_ids, "known_tails": known_tails}


def reference(entity_table, phases, head_owner, head_row, relation, tail_ids, known_tails):
    table_f = entity_table.astype(jnp.float32)
    table_sq = jnp.sum(table_f * table_f, axis=1)
    columns = jnp.arange(ENTITIES, dtype=jnp.int32)
    blocks_n = TRIPLES // TRIP_DEV

    def one_block(carry, index_b):
        grad_acc, rel_acc = carry
        start = (index_b * TRIP_DEV).astype(jnp.int32)
        owners = lax.dynamic_slice_in_dim(head_owner[:, 0], start, TRIP_DEV)
        rows_in = lax.dynamic_slice_in_dim(head_row, start, TRIP_DEV)
        rel_local = lax.dynamic_slice_in_dim(relation, start, TRIP_DEV)
        targets = lax.dynamic_slice_in_dim(tail_ids, start, TRIP_DEV)
        listed_ids = lax.dynamic_slice_in_dim(known_tails, start, TRIP_DEV, 0)
        heads = (owners * ROWS_OWN + rows_in).astype(jnp.int32)
        rel_glob = ((index_b % N_REL) * REL_GRP + rel_local).astype(jnp.int32)
        head_f = table_f[heads]
        angles = phases[rel_glob]
        cosine = jnp.cos(angles)
        sine_part = jnp.sin(angles)
        head_re = head_f[:, :DIM]
        head_im = head_f[:, DIM:]
        query_re = head_re * cosine - head_im * sine_part
        query_im = head_re * sine_part + head_im * cosine
        query = jnp.concatenate([query_re, query_im], axis=1).astype(jnp.bfloat16)
        query_f = query.astype(jnp.float32)
        query_sq = jnp.sum(query_f * query_f, axis=1)
        cross = jnp.dot(query, entity_table.T, preferred_element_type=jnp.float32)
        scores = 2.0 * cross - query_sq[:, None] - table_sq[None, :]
        listed = jnp.zeros((TRIP_DEV, ENTITIES), jnp.bool_)
        for column_j in range(LISTED):
            listed = listed | (listed_ids[:, column_j:column_j + 1] == columns[None, :])
        masked = listed & (columns[None, :] != targets[:, None])
        row_max = jnp.max(jnp.where(masked, -jnp.inf, scores), axis=1)
        raw_prob = jnp.where(masked, 0.0, jnp.exp(scores - row_max[:, None]))
        prob = raw_prob / jnp.sum(raw_prob, axis=1, keepdims=True)
        onehot = (columns[None, :] == targets[:, None]).astype(jnp.float32)
        weights = (prob - onehot).astype(jnp.bfloat16)
        dquery = 2.0 * jnp.dot(weights, entity_table, preferred_element_type=jnp.float32)
        grad_re = dquery[:, :DIM]
        grad_im = dquery[:, DIM:]
        head_rows = jnp.concatenate([grad_re * cosine + grad_im * sine_part, -grad_re * sine_part + grad_im * cosine], axis=1).astype(jnp.bfloat16)
        dangle = -query_im * grad_re + query_re * grad_im
        cross_t = lax.dot_general(weights, query, (((0,), (0,)), ((), ())), preferred_element_type=jnp.float32)
        counts = jnp.sum(weights.astype(jnp.float32), axis=0)
        term = 2.0 * (cross_t - counts[:, None] * table_f)
        head_term = jax.ops.segment_sum(head_rows.astype(jnp.float32), heads, num_segments=ENTITIES)
        rel_term = jax.ops.segment_sum(dangle, rel_glob, num_segments=RELS)
        return (grad_acc + term + head_term, rel_acc + rel_term), None

    start_carry = (jnp.zeros((ENTITIES, WIDTH), jnp.float32), jnp.zeros((RELS, DIM), jnp.float32))
    (entity_gradient, relation_gradient), unused = lax.scan(one_block, start_carry, jnp.arange(blocks_n, dtype=jnp.int32))
    return entity_gradient, relation_gradient
```

```python
import functools

import jax
import jax.numpy as jnp
from jax import lax
from jax.experimental import pallas as pl
from jax.experimental.pallas import tpu as pltpu
from jax.sharding import PartitionSpec as P

F32 = jnp.float32
BF16 = jnp.bfloat16
I32 = jnp.int32
VMEM_BYTES = 40 * 1024 * 1024
NT = (((1,), (1,)), ((), ()))

SIN_C = (0.9999999957, -0.1666665799, 0.008333051133, -0.0001980908535, 2.605256611e-06)
COS_C = (0.9999999998, -0.4999999936, 0.04166663628, -0.00138883618, 2.476018568e-05, -2.605198025e-07)


def params():
    return pltpu.CompilerParams(vmem_limit_bytes=VMEM_BYTES)


def cost(flops, nbytes, trans=0):
    return pl.CostEstimate(flops=flops, bytes_accessed=nbytes, transcendentals=trans)


def horner(coeffs, y):
    acc = jnp.full_like(y, coeffs[-1])
    for c in coeffs[-2::-1]:
        acc = acc * y + c
    return acc


def prepare_kernel(flip_ref, angles_ref, owner_ref, row_ref, tail_ref, known_ref, cos_ref, sin_ref, code_ref, *, owner_rows):
    u = angles_ref[...] * 0.5
    y = u * u
    s = u * horner(SIN_C, y)
    c = horner(COS_C, y)
    sin_ref[...] = 2.0 * s * c
    cos_ref[...] = 1.0 - 2.0 * s * s
    flip = flip_ref[0]
    n = owner_ref.shape[1]
    entities = code_ref.shape[1]
    heads = (owner_ref[...] * owner_rows + row_ref[...]) ^ flip
    tails = tail_ref[...] ^ flip
    known = known_ref[...] ^ flip
    bits = lax.shift_left(jnp.ones_like(known), known & 31)
    word_of = lax.shift_right_logical(known, 5)
    sub = lax.broadcasted_iota(I32, (8, n), 0)
    pieces = []
    for w in range(entities // 32):
        hit = jnp.where(word_of == w, bits, 0)
        word = hit[0:8]
        for r in range(8, hit.shape[0], 8):
            word = word | hit[r : r + 8]
        for shift in (4, 2, 1):
            word = word | pltpu.roll(word, shift, 0)
        for g in range(4):
            e = sub + (32 * w + 8 * g)
            listed = lax.shift_right_logical(word, sub + 8 * g) & 1
            target = jnp.where(e == tails, 1, 0)
            head = jnp.where(e == heads, 4, 0)
            pieces.append((listed & (1 - target)) | (target * 2) | head)
    code_ref[...] = jnp.concatenate(pieces, axis=0).T


def score_kernel(par_ref, *refs, peers):
    table_refs = refs[:peers]
    cos_ref, sin_ref, code_ref, keep_ref, send_ref, w_ref, q_ref, hr_ref, table, tsq = refs[peers:]
    half = cos_ref.shape[1]

    @pl.when(pl.program_id(0) == 0)
    def _():
        step = table_refs[0].shape[0]
        for i in range(peers):
            block = table_refs[i][...]
            table[i * step : (i + 1) * step, :] = block
        f = table[...].astype(F32)
        norm = jnp.sum(f * f, axis=1, keepdims=True)
        tsq[...] = jnp.broadcast_to(norm, (norm.shape[0], 128)).T[0:8]

    tab = table[...]
    cosine = cos_ref[...]
    sine = sin_ref[...]
    code = code_ref[...]
    hot = jnp.where((code & 4) != 0, 1.0, 0.0).astype(BF16)
    head = jnp.dot(hot, tab, preferred_element_type=F32)
    hre = head[:, :half]
    him = head[:, half:]
    qre = hre * cosine - him * sine
    qim = hre * sine + him * cosine
    q = jnp.concatenate([qre, qim], axis=1).astype(BF16)
    q_ref[...] = q
    qf = q.astype(F32)
    qsq = jnp.sum(qf * qf, axis=1, keepdims=True)
    cross = lax.dot_general(q, tab, NT, preferred_element_type=F32)
    scores = 2.0 * cross - qsq - tsq[0:1, :]
    masked = (code & 1) != 0
    target = jnp.where((code & 2) != 0, 1.0, 0.0)
    row_max = jnp.max(jnp.where(masked, -jnp.inf, scores), axis=1, keepdims=True)
    raw = jnp.where(masked, 0.0, jnp.exp(scores - row_max))
    prob = raw / jnp.sum(raw, axis=1, keepdims=True)
    w = (prob - target).astype(BF16)
    w_ref[...] = w
    dq = 2.0 * jnp.dot(w, tab, preferred_element_type=F32)
    dre = dq[:, :half]
    dim = dq[:, half:]
    dangle = (qre * dim - qim * dre).astype(BF16)
    quarter = half // 2
    first = dangle[:, :quarter]
    second = dangle[:, quarter:]
    even = par_ref[0] == 0
    keep_ref[...] = jnp.where(even, first, second)
    send_ref[...] = jnp.where(even, second, first)
    hr_ref[...] = jnp.concatenate([dre * cosine + dim * sine, dim * cosine - dre * sine], axis=1).astype(BF16)


def entity_kernel(pos_ref, w_ref, q_ref, hr_ref, owner_ref, row_ref, *refs, peers, n_rel, owner_rows):
    table_refs = refs[:peers]
    keep_ref, send_ref, wt, hot, counts, sel = refs[peers:]
    entities = w_ref.shape[1]
    n = w_ref.shape[0]

    @pl.when(pl.program_id(0) == 0)
    def _():
        def row_id(i):
            j = i % owner_rows
            p = (i // owner_rows) % peers
            k = (i // (owner_rows * peers)) % n_rel
            b = i // (owner_rows * peers * n_rel)
            return ((p * 2 + b) * n_rel + (k ^ pos_ref[1])) * owner_rows + j

        e = row_id(lax.broadcasted_iota(I32, (entities, entities), 0))
        pick = jnp.where(e == lax.broadcasted_iota(I32, (entities, entities), 1), 1.0, 0.0).astype(BF16)
        sel[...] = pick
        wtf = lax.dot_general(pick, w_ref[...], NT, preferred_element_type=F32)
        wt[...] = wtf.astype(BF16)
        counts[...] = jnp.broadcast_to(jnp.sum(wtf, axis=1, keepdims=True), counts.shape)
        heads = (owner_ref[...] * owner_rows + row_ref[...]) ^ pos_ref[0]
        eh = row_id(lax.broadcasted_iota(I32, (entities, n), 0))
        hot[...] = jnp.where(eh == heads, 1.0, 0.0).astype(BF16)

    tab = jnp.concatenate([r[...] for r in table_refs], axis=0)
    tab = jnp.dot(sel[...], tab, preferred_element_type=F32)
    cross = jnp.dot(wt[...], q_ref[...], preferred_element_type=F32)
    heads_sum = jnp.dot(hot[...], hr_ref[...], preferred_element_type=F32)
    total = 2.0 * (cross - counts[:, 0:1] * tab) + heads_sum
    keep_ref[...] = total[: entities // 2]
    send_ref[...] = total[entities // 2 :]


def scatter_kernel(chip_ref, mine_ref, theirs_ref, keep_ref, got_ref, *outs, peers, rows):
    ids = jnp.concatenate([mine_ref[...], theirs_ref[...]], axis=1)
    d = jnp.concatenate([keep_ref[...], got_ref[...]], axis=0)
    n = ids.shape[1]
    iota = lax.broadcasted_iota(I32, (rows, n), 0)
    for p in range(peers):
        base = (chip_ref[0] ^ p) * rows
        hot = jnp.where(iota == ids - base, 1.0, 0.0).astype(BF16)
        outs[p][...] = jnp.dot(hot, d, preferred_element_type=F32).astype(outs[p].dtype)


def place_kernel(pos_ref, *refs, peers, rows):
    out_ref = refs[-1]
    quarter = refs[0].shape[1]
    chip, par = pos_ref[0], pos_ref[1]
    for side in range(2):
        col = pl.multiple_of((par ^ side) * quarter, quarter)
        for p in range(peers):
            row = pl.multiple_of((chip ^ p) * rows, rows)
            out_ref[pl.ds(row, rows), pl.ds(col, quarter)] = refs[side * peers + p][...].astype(F32)


def local(entity_table, phases, head_owner, head_row, relation, tail_ids, known_tails):
    n_ent = lax.axis_size("ent")
    n_rel = lax.axis_size("rel")
    peers = n_ent // 2
    n = head_row.shape[0]
    rows_ent, width = entity_table.shape
    owner_rows = rows_ent // n_rel
    entities = rows_ent * n_ent
    half = width // 2
    quarter = half // 2
    rels = phases.shape[0]
    rows = rels // peers
    block = min(128, n)
    steps = n // block
    me_ent = lax.axis_index("ent")
    me_rel = lax.axis_index("rel")

    def swap(x, k):
        return lax.ppermute(x, "ent", [(i, i ^ k) for i in range(n_ent)])

    def swap_rel(x, k):
        return lax.ppermute(x, "rel", [(i, i ^ k) for i in range(n_rel)])

    smem = pl.BlockSpec(memory_space=pltpu.SMEM)

    owner_l = head_owner.reshape(1, n)
    row_l = head_row.reshape(1, n)
    rel_l = relation.reshape(1, n)
    tail_l = tail_ids.reshape(1, n)
    known_l = known_tails.T
    rel_mate = swap(rel_l, 1)
    pair = jnp.concatenate([entity_table, swap(entity_table, 1)], axis=0)
    tables = [pair] + [swap(pair, 2 * p) for p in range(1, peers)]

    flip = (me_ent * rows_ent).astype(I32)
    chip = (me_ent // 2).astype(I32)
    par = (me_ent % 2).astype(I32)

    angles = phases.at[relation].get(mode="promise_in_bounds")
    lane = lambda r: pl.BlockSpec((r, block), lambda i: (0, i))
    line = lambda c: pl.BlockSpec((block, c), lambda i: (i, 0))
    cosine, sine, code = pl.pallas_call(
        functools.partial(prepare_kernel, owner_rows=owner_rows),
        grid=(steps,),
        in_specs=[smem, line(half), lane(1), lane(1), lane(1), lane(known_l.shape[0])],
        out_specs=[line(half), line(half), line(entities)],
        out_shape=[
            jax.ShapeDtypeStruct((n, half), F32),
            jax.ShapeDtypeStruct((n, half), F32),
            jax.ShapeDtypeStruct((n, entities), I32),
        ],
        compiler_params=params(),
        cost_estimate=cost(30 * n * half, 12 * n * half),
        name="prepare",
    )(flip.reshape(1), angles, owner_l, row_l, tail_l, known_l)

    whole = lambda a: pl.BlockSpec(a.shape, lambda i: (0, 0))
    keep, send, w, q, hr = pl.pallas_call(
        functools.partial(score_kernel, peers=peers),
        grid=(steps,),
        in_specs=[smem] + [whole(t) for t in tables] + [line(half), line(half), line(entities)],
        out_specs=[line(quarter), line(quarter), line(entities), line(width), line(width)],
        out_shape=[
            jax.ShapeDtypeStruct((n, quarter), BF16),
            jax.ShapeDtypeStruct((n, quarter), BF16),
            jax.ShapeDtypeStruct((n, entities), BF16),
            jax.ShapeDtypeStruct((n, width), BF16),
            jax.ShapeDtypeStruct((n, width), BF16),
        ],
        scratch_shapes=[pltpu.VMEM((entities, width), BF16), pltpu.VMEM((8, entities), F32)],
        compiler_params=params(),
        cost_estimate=cost(6 * n * entities * width, 12 * n * width),
        name="score",
    )(par.reshape(1), *tables, cosine, sine, code)

    got = swap(send, 1)

    cols = 256 if width % 256 == 0 else width
    col = lambda r: pl.BlockSpec((r, cols), lambda i: (0, i))
    fixed = lambda r, c: pl.BlockSpec((r, c), lambda i: (0, 0))
    ent_keep, ent_send = pl.pallas_call(
        functools.partial(entity_kernel, peers=peers, n_rel=n_rel, owner_rows=owner_rows),
        grid=(width // cols,),
        in_specs=[smem, fixed(n, entities), col(n), col(n), fixed(1, n), fixed(1, n)] + [col(2 * rows_ent)] * peers,
        out_specs=[col(entities // 2), col(entities // 2)],
        out_shape=[jax.ShapeDtypeStruct((entities // 2, width), F32)] * 2,
        scratch_shapes=[
            pltpu.VMEM((entities, n), BF16),
            pltpu.VMEM((entities, n), BF16),
            pltpu.VMEM((entities, 128), F32),
            pltpu.VMEM((entities, entities), BF16),
        ],
        compiler_params=params(),
        cost_estimate=cost(4 * n * entities * width, 4 * n * width + 4 * entities * width),
        name="entity",
    )(jnp.stack([flip, me_rel.astype(I32)]), w, q, hr, owner_l, row_l, *tables)

    vm = pl.BlockSpec(memory_space=pltpu.VMEM)
    parts = pl.pallas_call(
        functools.partial(scatter_kernel, peers=peers, rows=rows),
        in_specs=[smem, vm, vm, vm, vm],
        out_specs=[vm] * peers,
        out_shape=[jax.ShapeDtypeStruct((rows, quarter), F32 if p == 0 else BF16) for p in range(peers)],
        compiler_params=params(),
        cost_estimate=cost(4 * n * rels * quarter, 4 * n * quarter + 2 * rels * quarter),
        name="scatter",
    )(chip.reshape(1), rel_l, rel_mate, keep, got)

    total = parts[0]
    for p in range(1, peers):
        total = total + swap(parts[p], 2 * p).astype(F32)
    final = total.astype(BF16)
    mine = [final] + [swap(final, 2 * p) for p in range(1, peers)]
    theirs = [swap(x, 1) for x in mine]
    relation_gradient = pl.pallas_call(
        functools.partial(place_kernel, peers=peers, rows=rows),
        in_specs=[smem] + [vm] * (2 * peers),
        out_specs=vm,
        out_shape=jax.ShapeDtypeStruct((rels, half), F32),
        compiler_params=params(),
        cost_estimate=cost(rels * half, 6 * rels * half),
        name="place",
    )(jnp.stack([chip, par]), *mine, *theirs)

    ent = ent_keep + swap(ent_send, 1)
    ent = ent.reshape(n_rel, peers * owner_rows, width)
    acc = ent[0]
    for k in range(1, n_rel):
        acc = acc + swap_rel(ent[k], k)
    acc = acc.reshape(peers, owner_rows, width)
    entity_gradient = acc[0]
    for p in range(1, peers):
        entity_gradient = entity_gradient + swap(acc[p], 2 * p)
    return entity_gradient, relation_gradient


def solution(mesh):
    in_specs = (
        P("ent", None),
        P("rel", None),
        P(("ent", "rel"), None),
        P(("ent", "rel")),
        P(("ent", "rel")),
        P(("ent", "rel")),
        P(("ent", "rel"), None),
    )
    out_specs = (P(("ent", "rel"), None), P("rel", None))
    return jax.shard_map(local, mesh=mesh, in_specs=in_specs, out_specs=out_specs, check_vma=False)
```

```python
import functools

import jax
import jax.numpy as jnp
from jax import lax
from jax.experimental import pallas as pl
from jax.experimental.pallas import tpu as pltpu
from jax.sharding import PartitionSpec as P

F32 = jnp.float32
BF16 = jnp.bfloat16
I32 = jnp.int32
VMEM_BYTES = 16 * 1024 * 1024
NT = (((1,), (1,)), ((), ()))

SIN_C = (0.9999999957, -0.1666665799, 0.008333051133, -0.0001980908535, 2.605256611e-06)
COS_C = (0.9999999998, -0.4999999936, 0.04166663628, -0.00138883618, 2.476018568e-05, -2.605198025e-07)


def params():
    return pltpu.CompilerParams(vmem_limit_bytes=VMEM_BYTES)


def cost(flops, nbytes, trans=0):
    return pl.CostEstimate(flops=flops, bytes_accessed=nbytes, transcendentals=trans)


def horner(coeffs, y):
    acc = jnp.full_like(y, coeffs[-1])
    for c in coeffs[-2::-1]:
        acc = acc * y + c
    return acc


def prepare_kernel(rel_hbm, phases_hbm, owner_hbm, row_hbm, tail_hbm, known_hbm, cos_ref, sin_ref, code_ref, rel_ref, phases_ref, owner_ref, row_ref, tail_ref, known_ref, sems, *, rows_ent, owner_rows):
    n = cos_ref.shape[0]
    copies = [
        pltpu.make_async_copy(src, dst, sems.at[i])
        for i, (src, dst) in enumerate(
            [
                (known_hbm, known_ref),
                (owner_hbm, owner_ref),
                (row_hbm, row_ref),
                (tail_hbm, tail_ref),
                (rel_hbm, rel_ref),
                (phases_hbm, phases_ref),
            ]
        )
    ]
    for copy in copies:
        copy.start()
    for copy in copies[:4]:
        copy.wait()
    flip = lax.axis_index("ent") * rows_ent
    entities = code_ref.shape[1]
    lanes = min(128, n)
    sub = lax.broadcasted_iota(I32, (8, lanes), 0)
    for start in range(0, n, lanes):
        at = slice(start, start + lanes)
        heads = (owner_ref[:, at] * owner_rows + row_ref[:, at]) ^ flip
        tails = tail_ref[:, at] ^ flip
        known = known_ref[:, at] ^ flip
        bits = lax.shift_left(jnp.ones_like(known), known & 31)
        word_of = lax.shift_right_logical(known, 5)
        pieces = []
        for w in range(entities // 32):
            hit = jnp.where(word_of == w, bits, 0)
            word = hit[0:8]
            for r in range(8, hit.shape[0], 8):
                word = word | hit[r : r + 8]
            for shift in (4, 2, 1):
                word = word | pltpu.roll(word, shift, 0)
            for g in range(4):
                e = sub + (32 * w + 8 * g)
                listed = lax.shift_right_logical(word, sub + 8 * g) & 1
                target = jnp.where(e == tails, 1, 0)
                head = jnp.where(e == heads, 4, 0)
                pieces.append((listed & (1 - target)) | (target * 2) | head)
        code_ref[at, :] = jnp.concatenate(pieces, axis=0).T

    for copy in copies[4:]:
        copy.wait()

    half = cos_ref.shape[1]
    place = lax.broadcasted_iota(I32, (8, half), 0)
    for start in range(0, n, 8):
        angle = jnp.broadcast_to(phases_ref[pl.ds(rel_ref[start], 1), :], (8, half))
        for j in range(1, 8):
            angle = jnp.where(place == j, jnp.broadcast_to(phases_ref[pl.ds(rel_ref[start + j], 1), :], (8, half)), angle)
        u = angle * 0.5
        y = u * u
        s = u * horner(SIN_C, y)
        t = 2.0 * s
        sin_ref[start : start + 8, :] = t * horner(COS_C, y)
        cos_ref[start : start + 8, :] = 1.0 - t * s


def score_kernel(*refs, peers, block):
    table_refs = refs[:peers]
    cos_ref, sin_ref, code_ref, keep_ref, send_ref, w_ref, q_ref = refs[peers:]
    n, half = cos_ref.shape
    quarter = half // 2
    tab = jnp.concatenate([r[...] for r in table_refs], axis=0)
    f = tab.astype(F32)
    norm = jnp.sum(f * f, axis=1, keepdims=True)
    tsq = jnp.broadcast_to(norm, (norm.shape[0], 128)).T[0:1]
    even = lax.axis_index("ent") % 2 == 0
    for start in range(0, n, block):
        at = slice(start, start + block)
        cosine = cos_ref[at, :]
        sine = sin_ref[at, :]
        code = code_ref[at, :]
        hot = jnp.where((code & 4) != 0, 1.0, 0.0).astype(BF16)
        head = jnp.dot(hot, tab, preferred_element_type=F32)
        hre = head[:, :half]
        him = head[:, half:]
        qre = hre * cosine - him * sine
        qim = hre * sine + him * cosine
        q = jnp.concatenate([qre, qim], axis=1).astype(BF16)
        q_ref[at, :] = q
        qf = q.astype(F32)
        qsq = jnp.sum(qf * qf, axis=1, keepdims=True)
        cross = lax.dot_general(q, tab, NT, preferred_element_type=F32)
        scores = 2.0 * cross - qsq - tsq
        masked = (code & 1) != 0
        target = jnp.where((code & 2) != 0, 1.0, 0.0)
        row_max = jnp.max(jnp.where(masked, -jnp.inf, scores), axis=1, keepdims=True)
        raw = jnp.where(masked, 0.0, jnp.exp(scores - row_max))
        prob = raw / jnp.sum(raw, axis=1, keepdims=True)
        w = (prob - target).astype(BF16)
        w_ref[at, :] = w
        dq = jnp.dot(w + w, tab, preferred_element_type=F32)
        dangle = (qre * dq[:, half:] - qim * dq[:, :half]).astype(BF16)
        first = dangle[:, :quarter]
        second = dangle[:, quarter:]
        keep_ref[at, :] = jnp.where(even, first, second)
        send_ref[at, :] = jnp.where(even, second, first)


def entity_kernel(w_ref, q_ref, cos_ref, sin_ref, owner_ref, row_ref, *refs, peers, n_rel, owner_rows, block):
    table_refs = refs[:peers]
    keep_ref, send_ref, hr = refs[peers:]
    n, entities = w_ref.shape
    half = cos_ref.shape[1]
    tab = jnp.concatenate([r[...] for r in table_refs], axis=0)
    for start in range(0, n, block):
        at = slice(start, start + block)
        w = w_ref[at, :]
        dq = jnp.dot(w + w, tab, preferred_element_type=F32)
        cosine = cos_ref[at, :]
        sine = sin_ref[at, :]
        dre = dq[:, :half]
        dim = dq[:, half:]
        hr[at, :half] = (dre * cosine + dim * sine).astype(BF16)
        hr[at, half:] = (dim * cosine - dre * sine).astype(BF16)

    flip = lax.axis_index("ent") * (n_rel * owner_rows)
    me_rel = lax.axis_index("rel")

    def row_id(i):
        at = i // owner_rows
        span = 2 * peers * n_rel
        rel_bit = jnp.zeros_like(i)
        span //= 2
        ent_bit = (at // span) & 1
        for bit in range(n_rel.bit_length() - 1):
            span //= 2
            rel_bit = rel_bit | (((at // span) & 1) << bit)
        for bit in range(1, peers.bit_length()):
            span //= 2
            ent_bit = ent_bit | (((at // span) & 1) << bit)
        return (ent_bit * n_rel + (rel_bit ^ me_rel)) * owner_rows + i % owner_rows

    e = row_id(lax.broadcasted_iota(I32, (entities, entities), 0))
    pick = jnp.where(e == lax.broadcasted_iota(I32, (entities, entities), 1), 1.0, 0.0).astype(BF16)
    wtf = lax.dot_general(pick, w_ref[...], NT, preferred_element_type=F32)
    counts = jnp.sum(wtf, axis=1, keepdims=True)
    heads = (owner_ref[...] * owner_rows + row_ref[...]) ^ flip
    eh = row_id(lax.broadcasted_iota(I32, (entities, n), 0))
    hot = jnp.where(eh == heads, 1.0, 0.0).astype(BF16)
    picked = jnp.dot(pick, tab, preferred_element_type=F32)
    cross = jnp.dot(wtf.astype(BF16), q_ref[...], preferred_element_type=F32)
    total = 2.0 * (cross - counts * picked) + jnp.dot(hot, hr[...], preferred_element_type=F32)
    keep_ref[...] = total[: entities // 2]
    send_ref[...] = total[entities // 2 :]


def scatter_kernel(mine_ref, theirs_ref, keep_ref, got_ref, *outs, peers, rows):
    chip = lax.axis_index("ent") // 2
    ids = jnp.concatenate([mine_ref[...], theirs_ref[...]], axis=1)
    d = jnp.concatenate([keep_ref[...], got_ref[...]], axis=0)
    n = ids.shape[1]
    iota = lax.broadcasted_iota(I32, (rows, n), 0)
    for p in range(peers):
        base = (chip ^ p) * rows
        hot = jnp.where(iota == ids - base, 1.0, 0.0).astype(BF16)
        outs[p][...] = jnp.dot(hot, d, preferred_element_type=F32).astype(outs[p].dtype)


def place_kernel(src_ref, *refs, side, peers, rows):
    if side:
        left_ref, right_ref, _, sum_ref, out_hbm, buf, sems = refs
    else:
        out_hbm, buf, sems = refs
    quarter = src_ref.shape[1]
    me = lax.axis_index("ent")
    chip, par = me // 2, me % 2
    col = pl.multiple_of((par ^ side) * quarter, quarter)
    copies = []
    for p in range(peers):
        row = pl.multiple_of((chip ^ p) * rows, rows)
        at = slice(p * rows, (p + 1) * rows)
        buf[at, :] = src_ref[at, :].astype(F32)
        copy = pltpu.make_async_copy(buf.at[at, :], out_hbm.at[pl.ds(row, rows), pl.ds(col, quarter)], sems.at[p])
        copy.start()
        copies.append(copy)
    if side:
        sum_ref[...] = left_ref[...] + right_ref[...]
    for copy in copies:
        copy.wait()


def local(entity_table, phases, head_owner, head_row, relation, tail_ids, known_tails):
    n_ent = lax.axis_size("ent")
    n_rel = lax.axis_size("rel")
    peers = n_ent // 2
    n = head_row.shape[0]
    rows_ent, width = entity_table.shape
    owner_rows = rows_ent // n_rel
    entities = rows_ent * n_ent
    half = width // 2
    quarter = half // 2
    rels = phases.shape[0]
    rows = rels // peers
    block = min(128, n)

    def swap(x, k):
        return lax.ppermute(x, "ent", [(i, i ^ k) for i in range(n_ent)])

    def swap_rel(x, k):
        return lax.ppermute(x, "rel", [(i, i ^ k) for i in range(n_rel)])

    hbm = pl.BlockSpec(memory_space=pltpu.HBM)

    owner_l = head_owner.reshape(1, n)
    row_l = head_row.reshape(1, n)
    rel_l = relation.reshape(1, n)
    tail_l = tail_ids.reshape(1, n)
    known_l = known_tails.T
    mate, rel_mate = lax.optimization_barrier((swap(entity_table, 1), swap(rel_l, 1)))
    pair = jnp.concatenate([entity_table, mate], axis=0)
    tables = [pair] + [swap(pair, 2 * p) for p in range(1, peers)]

    vm = pl.BlockSpec(memory_space=pltpu.VMEM)
    cosine, sine, code = pl.pallas_call(
        functools.partial(prepare_kernel, rows_ent=rows_ent, owner_rows=owner_rows),
        in_specs=[hbm] * 6,
        out_specs=[vm] * 3,
        scratch_shapes=[
            pltpu.SMEM((n,), I32),
            pltpu.VMEM((rels, half), F32),
            pltpu.VMEM((1, n), I32),
            pltpu.VMEM((1, n), I32),
            pltpu.VMEM((1, n), I32),
            pltpu.VMEM(known_l.shape, I32),
            pltpu.SemaphoreType.DMA((6,)),
        ],
        out_shape=[
            jax.ShapeDtypeStruct((n, half), F32),
            jax.ShapeDtypeStruct((n, half), F32),
            jax.ShapeDtypeStruct((n, entities), I32),
        ],
        compiler_params=params(),
        cost_estimate=cost(30 * n * half, 12 * n * half),
        name="prepare",
    )(*[pltpu.with_memory_space_constraint(x, pltpu.HBM) for x in (relation, phases, owner_l, row_l, tail_l, known_l)])

    keep, send, w, q = pl.pallas_call(
        functools.partial(score_kernel, peers=peers, block=block),
        in_specs=[vm] * (peers + 3),
        out_specs=[vm] * 4,
        out_shape=[
            jax.ShapeDtypeStruct((n, quarter), BF16),
            jax.ShapeDtypeStruct((n, quarter), BF16),
            jax.ShapeDtypeStruct((n, entities), BF16),
            jax.ShapeDtypeStruct((n, width), BF16),
        ],
        compiler_params=params(),
        cost_estimate=cost(6 * n * entities * width, 12 * n * width),
        name="score",
    )(*tables, cosine, sine, code)

    got = swap(send, 1)
    ent_keep, ent_send = pl.pallas_call(
        functools.partial(entity_kernel, peers=peers, n_rel=n_rel, owner_rows=owner_rows, block=block),
        in_specs=[vm] * (6 + peers),
        out_specs=[vm] * 2,
        out_shape=[jax.ShapeDtypeStruct((entities // 2, width), F32)] * 2,
        scratch_shapes=[pltpu.VMEM((n, width), BF16)],
        compiler_params=params(),
        cost_estimate=cost(6 * n * entities * width, 4 * n * width + 4 * entities * width),
        name="entity",
    )(w, q, cosine, sine, owner_l, row_l, *tables)

    parts = pl.pallas_call(
        functools.partial(scatter_kernel, peers=peers, rows=rows),
        in_specs=[vm] * 4,
        out_specs=[vm] * peers,
        out_shape=[jax.ShapeDtypeStruct((rows, quarter), F32 if p == 0 else BF16) for p in range(peers)],
        compiler_params=params(),
        cost_estimate=cost(4 * n * rels * quarter, 4 * n * quarter + 2 * rels * quarter),
        name="scatter",
    )(rel_l, rel_mate, keep, got)

    *parts, ent_keep, ent_send = lax.optimization_barrier((*parts, ent_keep, ent_send))

    received = [swap(parts[p], 2 * p) for p in range(1, peers)]
    total = parts[0]
    for part in received:
        total = total + part.astype(F32)
    final = total.astype(BF16)

    def fold(x, move, sent):
        middle = x.shape[0] // 2
        return x[:middle], move(x[middle:].astype(sent)).astype(F32)

    left, right = fold(ent_keep + swap(ent_send, 1), lambda x: swap_rel(x, 1), BF16)
    final, left, right = lax.optimization_barrier((final, left, right))
    for bit in range(1, n_rel.bit_length() - 1):
        left, right = fold(left + right, lambda x: swap_rel(x, 1 << bit), BF16)
    for bit in range(1, peers.bit_length() - 1):
        left, right = fold(left + right, lambda x: swap(x, 1 << bit), F32)

    mine = jnp.concatenate([final] + [swap(final, 2 * p) for p in range(1, peers)], axis=0)
    mine, left, right = lax.optimization_barrier((mine, left, right))
    left, right = fold(left + right, lambda x: swap(x, peers), F32)
    theirs = swap(mine, 1)

    def place(side, *args):
        shape = jax.ShapeDtypeStruct((rels, half), F32)
        return pl.pallas_call(
            functools.partial(place_kernel, side=side, peers=peers, rows=rows),
            in_specs=[vm] * 3 + [hbm] if side else [vm],
            out_specs=(vm, hbm) if side else hbm,
            out_shape=(jax.ShapeDtypeStruct((owner_rows, width), F32), shape) if side else shape,
            scratch_shapes=[pltpu.VMEM((rels, quarter), F32), pltpu.SemaphoreType.DMA((peers,))],
            input_output_aliases={3: 1} if side else {},
            compiler_params=params(),
            cost_estimate=cost(rels * half, 6 * rels * half),
            name="place",
        )(*args)

    return place(1, theirs, left, right, place(0, mine))


def solution(mesh):
    in_specs = (
        P("ent", None),
        P("rel", None),
        P(("ent", "rel"), None),
        P(("ent", "rel")),
        P(("ent", "rel")),
        P(("ent", "rel")),
        P(("ent", "rel"), None),
    )
    out_specs = (P(("ent", "rel"), None), P("rel", None))
    return jax.shard_map(local, mesh=mesh, in_specs=in_specs, out_specs=out_specs, check_vma=False)
```

```python
import functools

import jax
import jax.numpy as jnp
from jax import lax
from jax.experimental import pallas as pl
from jax.experimental.pallas import tpu as pltpu
from jax.sharding import PartitionSpec as P

F32 = jnp.float32
BF16 = jnp.bfloat16
I32 = jnp.int32
VMEM_BYTES = 16 * 1024 * 1024
NT = (((1,), (1,)), ((), ()))

SIN_C = (0.9999999957, -0.1666665799, 0.008333051133, -0.0001980908535, 2.605256611e-06)
COS_C = (0.9999999998, -0.4999999936, 0.04166663628, -0.00138883618, 2.476018568e-05, -2.605198025e-07)


def params():
    return pltpu.CompilerParams(vmem_limit_bytes=VMEM_BYTES)


def cost(flops, nbytes, trans=0):
    return pl.CostEstimate(flops=flops, bytes_accessed=nbytes, transcendentals=trans)


def horner(coeffs, y):
    acc = jnp.full_like(y, coeffs[-1])
    for c in coeffs[-2::-1]:
        acc = acc * y + c
    return acc


def prepare_kernel(
    rel_hbm, phases_hbm, owner_hbm, row_hbm, tail_hbm, known_hbm, table_hbm, cos_ref, sin_ref, code_ref, own_ref,
    rel_ref, phases_ref, owner_ref, row_ref, tail_ref, known_ref, sems, *, rows_ent, owner_rows,
):
    n = cos_ref.shape[0]
    pairs = [(known_hbm, known_ref), (owner_hbm, owner_ref), (row_hbm, row_ref), (tail_hbm, tail_ref)]
    pairs += [(rel_hbm, rel_ref), (phases_hbm, phases_ref), (table_hbm, own_ref)]
    copies = [pltpu.make_async_copy(src, dst, sems.at[i]) for i, (src, dst) in enumerate(pairs)]
    for copy in copies:
        copy.start()
    for copy in copies[:4]:
        copy.wait()
    flip = lax.axis_index("ent") * rows_ent
    entities = code_ref.shape[1]
    lanes = min(128, n)
    sub = lax.broadcasted_iota(I32, (8, lanes), 0)
    for start in range(0, n, lanes):
        at = slice(start, start + lanes)
        heads = (owner_ref[:, at] * owner_rows + row_ref[:, at]) ^ flip
        tails = tail_ref[:, at] ^ flip
        known = known_ref[:, at] ^ flip
        bits = lax.shift_left(jnp.ones_like(known), known & 31)
        word_of = lax.shift_right_logical(known, 5)
        pieces = []
        for w in range(entities // 32):
            hit = jnp.where(word_of == w, bits, 0)
            word = hit[0:8]
            for r in range(8, hit.shape[0], 8):
                word = word | hit[r : r + 8]
            for shift in (4, 2, 1):
                word = word | pltpu.roll(word, shift, 0)
            for g in range(4):
                e = sub + (32 * w + 8 * g)
                listed = lax.shift_right_logical(word, sub + 8 * g) & 1
                target = jnp.where(e == tails, 1, 0)
                head = jnp.where(e == heads, 4, 0)
                pieces.append((listed & (1 - target)) | (target * 2) | head)
        code_ref[at, :] = jnp.concatenate(pieces, axis=0).T

    for copy in copies[4:]:
        copy.wait()
    half = cos_ref.shape[1]
    place = lax.broadcasted_iota(I32, (8, half), 0)
    for start in range(0, n, 8):
        angle = jnp.broadcast_to(phases_ref[pl.ds(rel_ref[start], 1), :], (8, half))
        for j in range(1, 8):
            angle = jnp.where(place == j, jnp.broadcast_to(phases_ref[pl.ds(rel_ref[start + j], 1), :], (8, half)), angle)
        u = angle * 0.5
        y = u * u
        s = u * horner(SIN_C, y)
        t = 2.0 * s
        sin_ref[start : start + 8, :] = t * horner(COS_C, y)
        cos_ref[start : start + 8, :] = 1.0 - t * s


def candidates(own_ref, mate_ref, peers):
    step = own_ref.shape[0] // peers
    blocks = [ref[p * step : (p + 1) * step, :] for p in range(peers) for ref in (own_ref, mate_ref)]
    return jnp.concatenate(blocks, axis=0)


def score_kernel(*refs, peers, block):
    own_ref, mate_ref, cos_ref, sin_ref, code_ref, keep_ref, send_ref, w_ref, q_ref = refs
    n, half = cos_ref.shape
    quarter = half // 2
    tab = candidates(own_ref, mate_ref, peers)
    f = tab.astype(F32)
    norm = jnp.sum(f * f, axis=1, keepdims=True)
    tsq = jnp.broadcast_to(norm, (norm.shape[0], 128)).T[0:1]
    even = lax.axis_index("ent") % 2 == 0
    for start in range(0, n, block):
        at = slice(start, start + block)
        cosine = cos_ref[at, :]
        sine = sin_ref[at, :]
        code = code_ref[at, :]
        hot = jnp.where((code & 4) != 0, 1.0, 0.0).astype(BF16)
        head = jnp.dot(hot, tab, preferred_element_type=F32)
        hre = head[:, :half]
        him = head[:, half:]
        qre = hre * cosine - him * sine
        qim = hre * sine + him * cosine
        q = jnp.concatenate([qre, qim], axis=1).astype(BF16)
        q_ref[at, :] = q
        qf = q.astype(F32)
        qsq = jnp.sum(qf * qf, axis=1, keepdims=True)
        cross = lax.dot_general(q, tab, NT, preferred_element_type=F32)
        scores = 2.0 * cross - qsq - tsq
        masked = (code & 1) != 0
        target = jnp.where((code & 2) != 0, 1.0, 0.0)
        row_max = jnp.max(jnp.where(masked, -jnp.inf, scores), axis=1, keepdims=True)
        raw = jnp.where(masked, 0.0, jnp.exp(scores - row_max))
        prob = raw / jnp.sum(raw, axis=1, keepdims=True)
        w = (prob - target).astype(BF16)
        w_ref[at, :] = w
        dq = jnp.dot(w + w, tab, preferred_element_type=F32)
        dangle = (qre * dq[:, half:] - qim * dq[:, :half]).astype(BF16)
        first = dangle[:, :quarter]
        second = dangle[:, quarter:]
        keep_ref[at, :] = jnp.where(even, first, second)
        send_ref[at, :] = jnp.where(even, second, first)


def entity_kernel(w_ref, q_ref, cos_ref, sin_ref, owner_ref, row_ref, *refs, peers, n_rel, owner_rows, block):
    own_ref, mate_ref, keep_ref, send_ref, hr = refs
    n, entities = w_ref.shape
    half = cos_ref.shape[1]
    tab = candidates(own_ref, mate_ref, peers)
    for start in range(0, n, block):
        at = slice(start, start + block)
        w = w_ref[at, :]
        dq = jnp.dot(w + w, tab, preferred_element_type=F32)
        cosine = cos_ref[at, :]
        sine = sin_ref[at, :]
        dre = dq[:, :half]
        dim = dq[:, half:]
        hr[at, :half] = (dre * cosine + dim * sine).astype(BF16)
        hr[at, half:] = (dim * cosine - dre * sine).astype(BF16)

    flip = lax.axis_index("ent") * (n_rel * owner_rows)
    me_rel = lax.axis_index("rel")

    def row_id(i):
        at = i // owner_rows
        ent_bit = (at // (peers * n_rel)) | ((at // 2 % peers) << 1)
        rel_bit = at & 1
        for bit in range(n_rel.bit_length() - 2, 0, -1):
            rel_bit = rel_bit | (((at // (peers << bit)) & 1) << bit)
        return (ent_bit * n_rel + (rel_bit ^ me_rel)) * owner_rows + i % owner_rows

    e = row_id(lax.broadcasted_iota(I32, (entities, entities), 0))
    pick = jnp.where(e == lax.broadcasted_iota(I32, (entities, entities), 1), 1.0, 0.0).astype(BF16)
    wtf = lax.dot_general(pick, w_ref[...], NT, preferred_element_type=F32)
    counts = jnp.sum(wtf, axis=1, keepdims=True)
    heads = (owner_ref[...] * owner_rows + row_ref[...]) ^ flip
    eh = row_id(lax.broadcasted_iota(I32, (entities, n), 0))
    hot = jnp.where(eh == heads, 1.0, 0.0).astype(BF16)
    picked = jnp.dot(pick, tab, preferred_element_type=F32)
    cross = jnp.dot(wtf.astype(BF16), q_ref[...], preferred_element_type=F32)
    total = 2.0 * (cross - counts * picked) + jnp.dot(hot, hr[...], preferred_element_type=F32)
    keep_ref[...] = total[: entities // 2]
    send_ref[...] = total[entities // 2 :]


def scatter_kernel(mine_ref, theirs_ref, keep_ref, got_ref, *outs, peers, rows):
    chip = lax.axis_index("ent") // 2
    ids = jnp.concatenate([mine_ref[...], theirs_ref[...]], axis=1)
    d = jnp.concatenate([keep_ref[...], got_ref[...]], axis=0)
    n = ids.shape[1]
    iota = lax.broadcasted_iota(I32, (rows, n), 0)
    for p in range(peers):
        base = (chip ^ p) * rows
        hot = jnp.where(iota == ids - base, 1.0, 0.0).astype(BF16)
        outs[p][...] = jnp.dot(hot, d, preferred_element_type=F32).astype(outs[p].dtype)


def combine_kernel(own_ref, *refs, peers, cols):
    got_refs, (left_ref, right_ref, keep_ref), outs = refs[: peers - 1], refs[peers - 1 : peers + 2], refs[peers + 2 :]
    rows = own_ref.shape[0]
    total = own_ref[...]
    for got_ref in got_refs:
        total = total + got_ref[...].astype(F32)
    final = total.astype(BF16)
    ent = left_ref[...] + right_ref[...].astype(F32)
    span = ent.shape[0] // peers
    for p in range(peers):
        outs[p][:rows, :] = final
        chunk = ent[p * span : (p + 1) * span]
        if p == 0:
            keep_ref[...] = chunk
        else:
            blocks = [chunk[:, i : i + cols] for i in range(0, chunk.shape[1], cols)]
            outs[p][rows:, :] = jnp.concatenate(blocks, axis=0).astype(BF16)


def collect_kernel(keep_ref, *refs, rows, cols):
    got_refs, (mine_ref, other_ref) = refs[:-2], refs[-2:]
    span, width = keep_ref.shape
    total = keep_ref[...]
    for got_ref in got_refs:
        extra = got_ref[rows:, :].astype(F32)
        total = total + jnp.concatenate([extra[i * span : (i + 1) * span] for i in range(width // cols)], axis=1)
    mine_ref[...] = total[: span // 2]
    other_ref[...] = total[span // 2 :]


def place_kernel(src_ref, *refs, side, peers, rows):
    out_hbm, buf, sems = refs[-3:]
    quarter = src_ref.shape[1]
    me = lax.axis_index("ent")
    chip, par = me // 2, me % 2
    col = pl.multiple_of((par ^ side) * quarter, quarter)
    copies = []
    for p in range(peers):
        row = pl.multiple_of((chip ^ p) * rows, rows)
        at = slice(p * rows, (p + 1) * rows)
        buf[at, :] = src_ref[at, :].astype(F32)
        copies.append(pltpu.make_async_copy(buf.at[at, :], out_hbm.at[pl.ds(row, rows), pl.ds(col, quarter)], sems.at[p]))
        copies[-1].start()
    for copy in copies:
        copy.wait()


def local(entity_table, phases, head_owner, head_row, relation, tail_ids, known_tails):
    n_ent = lax.axis_size("ent")
    n_rel = lax.axis_size("rel")
    peers = n_ent // 2
    n = head_row.shape[0]
    rows_ent, width = entity_table.shape
    owner_rows = rows_ent // n_rel
    entities = rows_ent * n_ent
    half = width // 2
    quarter = half // 2
    rels = phases.shape[0]
    rows = rels // peers
    block = min(512, n)

    def swap(x, k):
        return lax.ppermute(x, "ent", [(i, i ^ k) for i in range(n_ent)])

    def swap_each(xs, order):
        got = dict(zip(order, lax.optimization_barrier([swap(xs[p], 2 * p) for p in order])))
        return [got[p] for p in range(1, peers)]

    def hold(x):
        return pltpu.with_memory_space_constraint(x, pltpu.HBM)

    middle = [peers // 2] if peers > 1 else []
    near = [p for p in range(1, peers // 2)]
    far = [p for p in range(peers // 2 + 1, peers)]
    ORD = {"yxd": middle + near + far, "ydx": middle + far + near, "xyd": near + middle + far, "dyx": far + middle + near, "dxy": far + near + middle}

    def swap_rel(x, k):
        return lax.ppermute(x, "rel", [(i, i ^ k) for i in range(n_rel)])

    hbm = pl.BlockSpec(memory_space=pltpu.HBM)
    vm = pl.BlockSpec(memory_space=pltpu.VMEM)

    owner_l = head_owner.reshape(1, n)
    row_l = head_row.reshape(1, n)
    rel_l = relation.reshape(1, n)
    tail_l = tail_ids.reshape(1, n)
    known_l = known_tails.T
    far = swap_each([entity_table] * peers, ORD["yxd"])
    fetched = [relation, phases, owner_l, row_l, tail_l, known_l, entity_table]
    cosine, sine, code, own = pl.pallas_call(
        functools.partial(prepare_kernel, rows_ent=rows_ent, owner_rows=owner_rows),
        in_specs=[hbm] * len(fetched),
        out_specs=[vm] * 4,
        out_shape=[
            jax.ShapeDtypeStruct((n, half), F32),
            jax.ShapeDtypeStruct((n, half), F32),
            jax.ShapeDtypeStruct((n, entities), I32),
            jax.ShapeDtypeStruct(entity_table.shape, BF16),
        ],
        scratch_shapes=[pltpu.SMEM((n,), I32)]
        + [pltpu.VMEM(x.shape, x.dtype) for x in fetched[1:6]]
        + [pltpu.SemaphoreType.DMA((len(fetched),))],
        compiler_params=params(),
        cost_estimate=cost(30 * n * half, 12 * n * half),
        name="prepare",
    )(*[hold(x) for x in fetched])

    cosine, sine, code, own, *far = lax.optimization_barrier((cosine, sine, code, own, *far))
    held = jnp.concatenate([own, *far], axis=0)
    mate, rel_mate = lax.optimization_barrier((swap(held, 1), swap(rel_l, 1)))
    tables = [held, mate]
    keep, send, w, q = pl.pallas_call(
        functools.partial(score_kernel, peers=peers, block=block),
        in_specs=[vm] * 5,
        out_specs=[vm] * 4,
        out_shape=[
            jax.ShapeDtypeStruct((n, quarter), BF16),
            jax.ShapeDtypeStruct((n, quarter), BF16),
            jax.ShapeDtypeStruct((n, entities), BF16),
            jax.ShapeDtypeStruct((n, width), BF16),
        ],
        compiler_params=params(),
        cost_estimate=cost(6 * n * entities * width, 12 * n * width),
        name="score",
    )(*tables, cosine, sine, code)

    got = swap(send, 1)
    ent_keep, ent_send = pl.pallas_call(
        functools.partial(entity_kernel, peers=peers, n_rel=n_rel, owner_rows=owner_rows, block=block),
        in_specs=[vm] * 8,
        out_specs=[vm] * 2,
        out_shape=[jax.ShapeDtypeStruct((entities // 2, width), F32)] * 2,
        scratch_shapes=[pltpu.VMEM((n, width), BF16)],
        compiler_params=params(),
        cost_estimate=cost(6 * n * entities * width, 4 * n * width + 4 * entities * width),
        name="entity",
    )(w, q, cosine, sine, owner_l, row_l, *tables)

    parts = pl.pallas_call(
        functools.partial(scatter_kernel, peers=peers, rows=rows),
        in_specs=[vm] * 4,
        out_specs=[vm] * peers,
        out_shape=[jax.ShapeDtypeStruct((rows, quarter), F32 if p == 0 else BF16) for p in range(peers)],
        compiler_params=params(),
        cost_estimate=cost(4 * n * rels * quarter, 4 * n * quarter + 2 * rels * quarter),
        name="scatter",
    )(rel_l, rel_mate, keep, got)

    *parts, ent_keep, ent_send = lax.optimization_barrier((*parts, ent_keep, ent_send))

    received = swap_each(parts, ORD["ydx"])

    left, right = ent_keep, swap(ent_send, 1)
    for bit in range(n_rel.bit_length() - 2, 0, -1):
        middle = left.shape[0] // 2
        left, right = (left + right)[:middle], swap_rel((left + right)[middle:].astype(BF16), 1 << bit)
    span = 2 * owner_rows
    extra = span * width // quarter
    ent_own, *messages = pl.pallas_call(
        functools.partial(combine_kernel, peers=peers, cols=quarter),
        in_specs=[vm] * (peers + 2),
        out_specs=[vm] * (peers + 1),
        out_shape=[jax.ShapeDtypeStruct((span, width), F32), jax.ShapeDtypeStruct((rows, quarter), BF16)]
        + [jax.ShapeDtypeStruct((rows + extra, quarter), BF16)] * (peers - 1),
        compiler_params=params(),
        cost_estimate=cost(4 * rows * quarter, 16 * rows * quarter),
        name="combine",
    )(parts[0], *received, left, right)
    final, far = messages[0], swap_each(messages, ORD["dxy"])
    mine = jnp.concatenate([final] + [x[:rows] for x in far], axis=0)
    left, right = pl.pallas_call(
        functools.partial(collect_kernel, rows=rows, cols=quarter),
        in_specs=[vm] * peers,
        out_specs=[vm] * 2,
        out_shape=[jax.ShapeDtypeStruct((owner_rows, width), F32)] * 2,
        compiler_params=params(),
        cost_estimate=cost(peers * span * width, 4 * peers * span * width),
        name="collect",
    )(ent_own, *far)
    theirs = swap(mine, 1)
    right = swap_rel(right, 1)

    gradient = jax.ShapeDtypeStruct((rels, half), F32)

    def place(side, *args):
        return pl.pallas_call(
            functools.partial(place_kernel, side=side, peers=peers, rows=rows),
            in_specs=[vm, hbm][: len(args)],
            out_specs=hbm,
            out_shape=gradient,
            scratch_shapes=[pltpu.VMEM((rels, quarter), F32), pltpu.SemaphoreType.DMA((peers,))],
            input_output_aliases={1: 0} if side else {},
            compiler_params=params(),
            cost_estimate=cost(rels * half, 6 * rels * half),
            name="place",
        )(*args)

    relation_gradient = place(1, theirs, place(0, mine))
    relation_gradient, left, right = lax.optimization_barrier((relation_gradient, left, right))
    return left + right, relation_gradient


def solution(mesh):
    in_specs = (
        P("ent", None),
        P("rel", None),
        P(("ent", "rel"), None),
        P(("ent", "rel")),
        P(("ent", "rel")),
        P(("ent", "rel")),
        P(("ent", "rel"), None),
    )
    out_specs = (P(("ent", "rel"), None), P("rel", None))
    return jax.shard_map(local, mesh=mesh, in_specs=in_specs, out_specs=out_specs, check_vma=False)
```

```python
import functools

import jax
import jax.numpy as jnp
from jax import lax
from jax.experimental import pallas as pl
from jax.experimental.pallas import tpu as pltpu
from jax.sharding import PartitionSpec as P

F32 = jnp.float32
BF16 = jnp.bfloat16
I32 = jnp.int32
VMEM_BYTES = 16 * 1024 * 1024
NT = (((1,), (1,)), ((), ()))

SIN_C = (0.9999999957, -0.1666665799, 0.008333051133, -0.0001980908535, 2.605256611e-06)
COS_C = (0.9999999998, -0.4999999936, 0.04166663628, -0.00138883618, 2.476018568e-05, -2.605198025e-07)


def params():
    return pltpu.CompilerParams(vmem_limit_bytes=VMEM_BYTES)


def cost(flops, nbytes, trans=0):
    return pl.CostEstimate(flops=flops, bytes_accessed=nbytes, transcendentals=trans)


def horner(coeffs, y):
    acc = jnp.full_like(y, coeffs[-1])
    for c in coeffs[-2::-1]:
        acc = acc * y + c
    return acc


def prepare_kernel(
    rel_hbm, phases_hbm, owner_hbm, row_hbm, tail_hbm, known_hbm, table_hbm, cos_ref, sin_ref, code_ref, own_ref,
    rel_ref, phases_ref, owner_ref, row_ref, tail_ref, known_ref, sems, *, rows_ent, owner_rows,
):
    n = cos_ref.shape[0]
    pairs = [(known_hbm, known_ref), (owner_hbm, owner_ref), (row_hbm, row_ref), (tail_hbm, tail_ref)]
    pairs += [(rel_hbm, rel_ref), (phases_hbm, phases_ref), (table_hbm, own_ref)]
    copies = [pltpu.make_async_copy(src, dst, sems.at[i]) for i, (src, dst) in enumerate(pairs)]
    for copy in copies:
        copy.start()
    for copy in copies[:4]:
        copy.wait()
    flip = lax.axis_index("ent") * rows_ent
    entities = code_ref.shape[1]
    lanes = min(128, n)
    sub = lax.broadcasted_iota(I32, (8, lanes), 0)
    for start in range(0, n, lanes):
        at = slice(start, start + lanes)
        heads = (owner_ref[:, at] * owner_rows + row_ref[:, at]) ^ flip
        tails = tail_ref[:, at] ^ flip
        known = known_ref[:, at] ^ flip
        bits = lax.shift_left(jnp.ones_like(known), known & 31)
        word_of = lax.shift_right_logical(known, 5)
        pieces = []
        for w in range(entities // 32):
            hit = jnp.where(word_of == w, bits, 0)
            word = hit[0:8]
            for r in range(8, hit.shape[0], 8):
                word = word | hit[r : r + 8]
            for shift in (4, 2, 1):
                word = word | pltpu.roll(word, shift, 0)
            for g in range(4):
                e = sub + (32 * w + 8 * g)
                listed = lax.shift_right_logical(word, sub + 8 * g) & 1
                target = jnp.where(e == tails, 1, 0)
                head = jnp.where(e == heads, 4, 0)
                pieces.append((listed & (1 - target)) | (target * 2) | head)
        code_ref[at, :] = jnp.concatenate(pieces, axis=0).T

    for copy in copies[4:]:
        copy.wait()
    half = cos_ref.shape[1]
    place = lax.broadcasted_iota(I32, (8, half), 0)
    for start in range(0, n, 8):
        angle = jnp.broadcast_to(phases_ref[pl.ds(rel_ref[start], 1), :], (8, half))
        for j in range(1, 8):
            angle = jnp.where(place == j, jnp.broadcast_to(phases_ref[pl.ds(rel_ref[start + j], 1), :], (8, half)), angle)
        u = angle * 0.5
        y = u * u
        s = u * horner(SIN_C, y)
        t = 2.0 * s
        sin_ref[start : start + 8, :] = t * horner(COS_C, y)
        cos_ref[start : start + 8, :] = 1.0 - t * s


def candidates(own_ref, mate_ref, peers):
    step = own_ref.shape[0] // peers
    blocks = [ref[p * step : (p + 1) * step, :] for p in range(peers) for ref in (own_ref, mate_ref)]
    return jnp.concatenate(blocks, axis=0)


def score_kernel(*refs, peers, block):
    own_ref, mate_ref, cos_ref, sin_ref, code_ref, keep_ref, send_ref, w_ref, q_ref = refs
    n, half = cos_ref.shape
    quarter = half // 2
    tab = candidates(own_ref, mate_ref, peers)
    f = tab.astype(F32)
    norm = jnp.sum(f * f, axis=1, keepdims=True)
    tsq = jnp.broadcast_to(norm, (norm.shape[0], 128)).T[0:1]
    even = lax.axis_index("ent") % 2 == 0
    for start in range(0, n, block):
        at = slice(start, start + block)
        cosine = cos_ref[at, :]
        sine = sin_ref[at, :]
        code = code_ref[at, :]
        hot = jnp.where((code & 4) != 0, 1.0, 0.0).astype(BF16)
        head = jnp.dot(hot, tab, preferred_element_type=F32)
        hre = head[:, :half]
        him = head[:, half:]
        qre = hre * cosine - him * sine
        qim = hre * sine + him * cosine
        q = jnp.concatenate([qre, qim], axis=1).astype(BF16)
        q_ref[at, :] = q
        qf = q.astype(F32)
        qsq = jnp.sum(qf * qf, axis=1, keepdims=True)
        cross = lax.dot_general(q, tab, NT, preferred_element_type=F32)
        scores = 2.0 * cross - qsq - tsq
        masked = (code & 1) != 0
        target = jnp.where((code & 2) != 0, 1.0, 0.0)
        row_max = jnp.max(jnp.where(masked, -jnp.inf, scores), axis=1, keepdims=True)
        raw = jnp.where(masked, 0.0, jnp.exp(scores - row_max))
        prob = raw / jnp.sum(raw, axis=1, keepdims=True)
        w = (prob - target).astype(BF16)
        w_ref[at, :] = w
        dq = jnp.dot(w + w, tab, preferred_element_type=F32)
        dangle = (qre * dq[:, half:] - qim * dq[:, :half]).astype(BF16)
        first = dangle[:, :quarter]
        second = dangle[:, quarter:]
        keep_ref[at, :] = jnp.where(even, first, second)
        send_ref[at, :] = jnp.where(even, second, first)


def entity_kernel(w_ref, q_ref, cos_ref, sin_ref, owner_ref, row_ref, *refs, peers, n_rel, owner_rows, block):
    own_ref, mate_ref, keep_ref, send_ref, hr = refs
    n, entities = w_ref.shape
    half = cos_ref.shape[1]
    tab = candidates(own_ref, mate_ref, peers)
    for start in range(0, n, block):
        at = slice(start, start + block)
        w = w_ref[at, :]
        dq = jnp.dot(w + w, tab, preferred_element_type=F32)
        cosine = cos_ref[at, :]
        sine = sin_ref[at, :]
        dre = dq[:, :half]
        dim = dq[:, half:]
        hr[at, :half] = (dre * cosine + dim * sine).astype(BF16)
        hr[at, half:] = (dim * cosine - dre * sine).astype(BF16)

    flip = lax.axis_index("ent") * (n_rel * owner_rows)
    me_rel = lax.axis_index("rel")

    def row_id(i):
        at = i // owner_rows
        ent_bit = (at // (peers * n_rel)) | ((at // 2 % peers) << 1)
        rel_bit = at & 1
        for bit in range(n_rel.bit_length() - 2, 0, -1):
            rel_bit = rel_bit | (((at // (peers << bit)) & 1) << bit)
        return (ent_bit * n_rel + (rel_bit ^ me_rel)) * owner_rows + i % owner_rows

    e = row_id(lax.broadcasted_iota(I32, (entities, entities), 0))
    pick = jnp.where(e == lax.broadcasted_iota(I32, (entities, entities), 1), 1.0, 0.0).astype(BF16)
    wtf = lax.dot_general(pick, w_ref[...], NT, preferred_element_type=F32)
    counts = jnp.sum(wtf, axis=1, keepdims=True)
    heads = (owner_ref[...] * owner_rows + row_ref[...]) ^ flip
    eh = row_id(lax.broadcasted_iota(I32, (entities, n), 0))
    hot = jnp.where(eh == heads, 1.0, 0.0).astype(BF16)
    picked = jnp.dot(pick, tab, preferred_element_type=F32)
    cross = jnp.dot(wtf.astype(BF16), q_ref[...], preferred_element_type=F32)
    total = 2.0 * (cross - counts * picked) + jnp.dot(hot, hr[...], preferred_element_type=F32)
    keep_ref[...] = total[: entities // 2]
    send_ref[...] = total[entities // 2 :]


def scatter_kernel(mine_ref, theirs_ref, keep_ref, got_ref, *outs, shares, rows):
    chip = lax.axis_index("ent") // 2
    ids = jnp.concatenate([mine_ref[...], theirs_ref[...]], axis=1)
    d = jnp.concatenate([keep_ref[...], got_ref[...]], axis=0)
    n = ids.shape[1]
    iota = lax.broadcasted_iota(I32, (rows, n), 0)
    for out, (p, first) in zip(outs, shares):
        base = (chip ^ p) * (rows * (2 if p == 0 else 1)) + first
        hot = jnp.where(iota == ids - base, 1.0, 0.0).astype(BF16)
        out[...] = jnp.dot(hot, d, preferred_element_type=F32).astype(out.dtype)


def combine_kernel(low_ref, high_ref, *refs, peers, cols):
    got_refs, (left_ref, right_ref, keep_ref), outs = refs[: peers - 1], refs[peers - 1 : peers + 2], refs[peers + 2 :]
    total = jnp.concatenate([low_ref[...], high_ref[...]], axis=0)
    rows = total.shape[0]
    for got_ref in got_refs:
        total = total + got_ref[...].astype(F32)
    final = total.astype(BF16)
    ent = left_ref[...] + right_ref[...].astype(F32)
    span = ent.shape[0] // peers
    for p in range(peers):
        outs[p][:rows, :] = final
        chunk = ent[p * span : (p + 1) * span]
        if p == 0:
            keep_ref[...] = chunk
        else:
            blocks = [chunk[:, i : i + cols] for i in range(0, chunk.shape[1], cols)]
            outs[p][rows:, :] = jnp.concatenate(blocks, axis=0).astype(BF16)


def collect_kernel(keep_ref, *refs, rows, cols):
    got_refs, (mine_ref, other_ref) = refs[:-2], refs[-2:]
    span, width = keep_ref.shape
    total = keep_ref[...]
    for got_ref in got_refs:
        extra = got_ref[rows:, :].astype(F32)
        total = total + jnp.concatenate([extra[i * span : (i + 1) * span] for i in range(width // cols)], axis=1)
    mine_ref[...] = total[: span // 2]
    other_ref[...] = total[span // 2 :]


def place_kernel(src_ref, *refs, side, peers, rows):
    out_hbm, buf, sems = refs[-3:]
    quarter = src_ref.shape[1]
    me = lax.axis_index("ent")
    chip, par = me // 2, me % 2
    col = pl.multiple_of((par ^ side) * quarter, quarter)
    copies = []
    for p in range(peers):
        row = pl.multiple_of((chip ^ p) * rows, rows)
        at = slice(p * rows, (p + 1) * rows)
        buf[at, :] = src_ref[at, :].astype(F32)
        copies.append(pltpu.make_async_copy(buf.at[at, :], out_hbm.at[pl.ds(row, rows), pl.ds(col, quarter)], sems.at[p]))
        copies[-1].start()
    for copy in copies:
        copy.wait()


def local(entity_table, phases, head_owner, head_row, relation, tail_ids, known_tails):
    n_ent = lax.axis_size("ent")
    n_rel = lax.axis_size("rel")
    peers = n_ent // 2
    n = head_row.shape[0]
    rows_ent, width = entity_table.shape
    owner_rows = rows_ent // n_rel
    entities = rows_ent * n_ent
    half = width // 2
    quarter = half // 2
    rels = phases.shape[0]
    rows = rels // peers
    block = min(512, n)

    def swap(x, k):
        return lax.ppermute(x, "ent", [(i, i ^ k) for i in range(n_ent)])

    def swap_each(xs, order):
        got = dict(zip(order, lax.optimization_barrier([swap(xs[p], 2 * p) for p in order])))
        return [got[p] for p in range(1, peers)]

    def hold(x):
        return pltpu.with_memory_space_constraint(x, pltpu.HBM)

    middle = [peers // 2] if peers > 1 else []
    near = [p for p in range(1, peers // 2)]
    far = [p for p in range(peers // 2 + 1, peers)]
    ORD = {"yxd": middle + near + far, "ydx": middle + far + near, "xyd": near + middle + far, "dyx": far + middle + near, "dxy": far + near + middle}

    def swap_rel(x, k):
        return lax.ppermute(x, "rel", [(i, i ^ k) for i in range(n_rel)])

    hbm = pl.BlockSpec(memory_space=pltpu.HBM)
    vm = pl.BlockSpec(memory_space=pltpu.VMEM)

    owner_l = head_owner.reshape(1, n)
    row_l = head_row.reshape(1, n)
    rel_l = relation.reshape(1, n)
    tail_l = tail_ids.reshape(1, n)
    known_l = known_tails.T
    far = swap_each([entity_table] * peers, ORD["yxd"])
    fetched = [relation, phases, owner_l, row_l, tail_l, known_l, entity_table]
    cosine, sine, code, own = pl.pallas_call(
        functools.partial(prepare_kernel, rows_ent=rows_ent, owner_rows=owner_rows),
        in_specs=[hbm] * len(fetched),
        out_specs=[vm] * 4,
        out_shape=[
            jax.ShapeDtypeStruct((n, half), F32),
            jax.ShapeDtypeStruct((n, half), F32),
            jax.ShapeDtypeStruct((n, entities), I32),
            jax.ShapeDtypeStruct(entity_table.shape, BF16),
        ],
        scratch_shapes=[pltpu.SMEM((n,), I32)]
        + [pltpu.VMEM(x.shape, x.dtype) for x in fetched[1:6]]
        + [pltpu.SemaphoreType.DMA((len(fetched),))],
        compiler_params=params(),
        cost_estimate=cost(30 * n * half, 12 * n * half),
        name="prepare",
    )(*[hold(x) for x in fetched])

    cosine, sine, code, own, *far = lax.optimization_barrier((cosine, sine, code, own, *far))
    held = jnp.concatenate([own, *far], axis=0)
    mate, rel_mate = lax.optimization_barrier((swap(held, 1), swap(rel_l, 1)))
    tables = [held, mate]
    keep, send, w, q = pl.pallas_call(
        functools.partial(score_kernel, peers=peers, block=block),
        in_specs=[vm] * 5,
        out_specs=[vm] * 4,
        out_shape=[
            jax.ShapeDtypeStruct((n, quarter), BF16),
            jax.ShapeDtypeStruct((n, quarter), BF16),
            jax.ShapeDtypeStruct((n, entities), BF16),
            jax.ShapeDtypeStruct((n, width), BF16),
        ],
        compiler_params=params(),
        cost_estimate=cost(6 * n * entities * width, 12 * n * width),
        name="score",
    )(*tables, cosine, sine, code)

    got = swap(send, 1)
    ent_keep, ent_send = pl.pallas_call(
        functools.partial(entity_kernel, peers=peers, n_rel=n_rel, owner_rows=owner_rows, block=block),
        in_specs=[vm] * 8,
        out_specs=[vm] * 2,
        out_shape=[jax.ShapeDtypeStruct((entities // 2, width), F32)] * 2,
        scratch_shapes=[pltpu.VMEM((n, width), BF16)],
        compiler_params=params(),
        cost_estimate=cost(6 * n * entities * width, 4 * n * width + 4 * entities * width),
        name="entity",
    )(w, q, cosine, sine, owner_l, row_l, *tables)

    def scatter(shares, rows, dtype, work):
        return pl.pallas_call(
            functools.partial(scatter_kernel, shares=shares, rows=rows),
            in_specs=[vm] * 4,
            out_specs=[vm] * len(shares),
            out_shape=[jax.ShapeDtypeStruct((rows, quarter), dtype)] * len(shares),
            compiler_params=params(),
            cost_estimate=work,
            name="scatter",
        )(rel_l, rel_mate, keep, got)

    parts = scatter([(p, 0) for p in range(1, peers)], rows, BF16, cost(4 * n * rels * quarter, 4 * n * quarter + 2 * rels * quarter))
    *parts, ent_keep, ent_send = lax.optimization_barrier((*parts, ent_keep, ent_send))

    parts = [None, *parts]
    low, = scatter([(0, 0)], rows // 2, F32, cost(10**9, 8 * n * quarter))
    high, = scatter([(0, rows // 2)], rows // 2, F32, cost(10**9, 8 * n * quarter))
    received = swap_each(parts, ORD["ydx"])

    left, right = ent_keep, swap(ent_send, 1)
    for bit in range(n_rel.bit_length() - 2, 0, -1):
        middle = left.shape[0] // 2
        left, right = (left + right)[:middle], swap_rel((left + right)[middle:].astype(BF16), 1 << bit)
    span = 2 * owner_rows
    extra = span * width // quarter
    ent_own, *messages = pl.pallas_call(
        functools.partial(combine_kernel, peers=peers, cols=quarter),
        in_specs=[vm] * (peers + 3),
        out_specs=[vm] * (peers + 1),
        out_shape=[jax.ShapeDtypeStruct((span, width), F32), jax.ShapeDtypeStruct((rows, quarter), BF16)]
        + [jax.ShapeDtypeStruct((rows + extra, quarter), BF16)] * (peers - 1),
        compiler_params=params(),
        cost_estimate=cost(4 * rows * quarter, 16 * rows * quarter),
        name="combine",
    )(low, high, *received, left, right)
    final, far = messages[0], swap_each(messages, ORD["dxy"])
    mine = jnp.concatenate([final] + [x[:rows] for x in far], axis=0)
    left, right = pl.pallas_call(
        functools.partial(collect_kernel, rows=rows, cols=quarter),
        in_specs=[vm] * peers,
        out_specs=[vm] * 2,
        out_shape=[jax.ShapeDtypeStruct((owner_rows, width), F32)] * 2,
        compiler_params=params(),
        cost_estimate=cost(peers * span * width, 4 * peers * span * width),
        name="collect",
    )(ent_own, *far)
    theirs = swap(mine, 1)
    right = swap_rel(right, 1)

    gradient = jax.ShapeDtypeStruct((rels, half), F32)

    def place(side, *args):
        return pl.pallas_call(
            functools.partial(place_kernel, side=side, peers=peers, rows=rows),
            in_specs=[vm, hbm][: len(args)],
            out_specs=hbm,
            out_shape=gradient,
            scratch_shapes=[pltpu.VMEM((rels, quarter), F32), pltpu.SemaphoreType.DMA((peers,))],
            input_output_aliases={1: 0} if side else {},
            compiler_params=params(),
            cost_estimate=cost(rels * half, 6 * rels * half),
            name="place",
        )(*args)

    relation_gradient = place(1, theirs, place(0, mine))
    relation_gradient, left, right = lax.optimization_barrier((relation_gradient, left, right))
    return left + right, relation_gradient


def solution(mesh):
    in_specs = (
        P("ent", None),
        P("rel", None),
        P(("ent", "rel"), None),
        P(("ent", "rel")),
        P(("ent", "rel")),
        P(("ent", "rel")),
        P(("ent", "rel"), None),
    )
    out_specs = (P(("ent", "rel"), None), P("rel", None))
    return jax.shard_map(local, mesh=mesh, in_specs=in_specs, out_specs=out_specs, check_vma=False)
```

```python
import functools

import jax
import jax.numpy as jnp
from jax import lax
from jax.experimental import pallas as pl
from jax.experimental.pallas import tpu as pltpu
from jax.sharding import PartitionSpec as P

F32 = jnp.float32
BF16 = jnp.bfloat16
I32 = jnp.int32
VMEM_BYTES = 16 * 1024 * 1024
NT = (((1,), (1,)), ((), ()))

SIN_C = (0.9999999957, -0.1666665799, 0.008333051133, -0.0001980908535, 2.605256611e-06)
COS_C = (0.9999999998, -0.4999999936, 0.04166663628, -0.00138883618, 2.476018568e-05, -2.605198025e-07)


def params():
    return pltpu.CompilerParams(vmem_limit_bytes=VMEM_BYTES)


def cost(flops, nbytes, trans=0):
    return pl.CostEstimate(flops=flops, bytes_accessed=nbytes, transcendentals=trans)


def horner(coeffs, y):
    acc = jnp.full_like(y, coeffs[-1])
    for c in coeffs[-2::-1]:
        acc = acc * y + c
    return acc


def prepare_kernel(
    rel_hbm, phases_hbm, owner_hbm, row_hbm, tail_hbm, known_hbm, table_hbm, cos_ref, sin_ref, code_ref, own_ref,
    rel_ref, phases_ref, owner_ref, row_ref, tail_ref, known_ref, sems, *, rows_ent, owner_rows,
):
    n = cos_ref.shape[0]
    pairs = [(known_hbm, known_ref), (owner_hbm, owner_ref), (row_hbm, row_ref), (tail_hbm, tail_ref)]
    pairs += [(rel_hbm, rel_ref), (phases_hbm, phases_ref), (table_hbm, own_ref)]
    copies = [pltpu.make_async_copy(src, dst, sems.at[i]) for i, (src, dst) in enumerate(pairs)]
    for copy in copies:
        copy.start()
    for copy in copies[:4]:
        copy.wait()
    flip = lax.axis_index("ent") * rows_ent
    entities = code_ref.shape[1]
    lanes = min(128, n)
    sub = lax.broadcasted_iota(I32, (8, lanes), 0)
    for start in range(0, n, lanes):
        at = slice(start, start + lanes)
        heads = (owner_ref[:, at] * owner_rows + row_ref[:, at]) ^ flip
        tails = tail_ref[:, at] ^ flip
        known = known_ref[:, at] ^ flip
        bits = lax.shift_left(jnp.ones_like(known), known & 31)
        word_of = lax.shift_right_logical(known, 5)
        pieces = []
        for w in range(entities // 32):
            hit = jnp.where(word_of == w, bits, 0)
            word = hit[0:8]
            for r in range(8, hit.shape[0], 8):
                word = word | hit[r : r + 8]
            for shift in (4, 2, 1):
                word = word | pltpu.roll(word, shift, 0)
            for g in range(4):
                e = sub + (32 * w + 8 * g)
                listed = lax.shift_right_logical(word, sub + 8 * g) & 1
                target = jnp.where(e == tails, 1, 0)
                head = jnp.where(e == heads, 4, 0)
                pieces.append((listed & (1 - target)) | (target * 2) | head)
        code_ref[at, :] = jnp.concatenate(pieces, axis=0).T

    for copy in copies[4:]:
        copy.wait()
    half = cos_ref.shape[1]
    place = lax.broadcasted_iota(I32, (8, half), 0)
    for start in range(0, n, 8):
        angle = jnp.broadcast_to(phases_ref[pl.ds(rel_ref[start], 1), :], (8, half))
        for j in range(1, 8):
            angle = jnp.where(place == j, jnp.broadcast_to(phases_ref[pl.ds(rel_ref[start + j], 1), :], (8, half)), angle)
        u = angle * 0.5
        y = u * u
        s = u * horner(SIN_C, y)
        t = 2.0 * s
        sin_ref[start : start + 8, :] = t * horner(COS_C, y)
        cos_ref[start : start + 8, :] = 1.0 - t * s


def candidates(own_ref, mate_ref, peers):
    step = own_ref.shape[0] // peers
    blocks = [ref[p * step : (p + 1) * step, :] for p in range(peers) for ref in (own_ref, mate_ref)]
    return jnp.concatenate(blocks, axis=0)


def score_kernel(*refs, peers, block):
    own_ref, mate_ref, cos_ref, sin_ref, code_ref, keep_ref, send_ref, w_ref, q_ref = refs
    n, half = cos_ref.shape
    quarter = half // 2
    tab = candidates(own_ref, mate_ref, peers)
    f = tab.astype(F32)
    norm = jnp.sum(f * f, axis=1, keepdims=True)
    tsq = jnp.broadcast_to(norm, (norm.shape[0], 128)).T[0:1]
    even = lax.axis_index("ent") % 2 == 0
    for start in range(0, n, block):
        at = slice(start, start + block)
        cosine = cos_ref[at, :]
        sine = sin_ref[at, :]
        code = code_ref[at, :]
        hot = jnp.where((code & 4) != 0, 1.0, 0.0).astype(BF16)
        head = jnp.dot(hot, tab, preferred_element_type=F32)
        hre = head[:, :half]
        him = head[:, half:]
        qre = hre * cosine - him * sine
        qim = hre * sine + him * cosine
        q = jnp.concatenate([qre, qim], axis=1).astype(BF16)
        q_ref[at, :] = q
        qf = q.astype(F32)
        qsq = jnp.sum(qf * qf, axis=1, keepdims=True)
        cross = lax.dot_general(q, tab, NT, preferred_element_type=F32)
        scores = 2.0 * cross - qsq - tsq
        masked = (code & 1) != 0
        target = jnp.where((code & 2) != 0, 1.0, 0.0)
        row_max = jnp.max(jnp.where(masked, -jnp.inf, scores), axis=1, keepdims=True)
        raw = jnp.where(masked, 0.0, jnp.exp(scores - row_max))
        prob = raw / jnp.sum(raw, axis=1, keepdims=True)
        w = (prob - target).astype(BF16)
        w_ref[at, :] = w
        dq = jnp.dot(w + w, tab, preferred_element_type=F32)
        dangle = (qre * dq[:, half:] - qim * dq[:, :half]).astype(BF16)
        first = dangle[:, :quarter]
        second = dangle[:, quarter:]
        keep_ref[at, :] = jnp.where(even, first, second)
        send_ref[at, :] = jnp.where(even, second, first)


def entity_kernel(w_ref, q_ref, cos_ref, sin_ref, owner_ref, row_ref, *refs, peers, n_rel, owner_rows, block):
    own_ref, mate_ref, keep_ref, send_ref, hr = refs
    n, entities = w_ref.shape
    half = cos_ref.shape[1]
    tab = candidates(own_ref, mate_ref, peers)
    for start in range(0, n, block):
        at = slice(start, start + block)
        w = w_ref[at, :]
        dq = jnp.dot(w + w, tab, preferred_element_type=F32)
        cosine = cos_ref[at, :]
        sine = sin_ref[at, :]
        dre = dq[:, :half]
        dim = dq[:, half:]
        hr[at, :half] = (dre * cosine + dim * sine).astype(BF16)
        hr[at, half:] = (dim * cosine - dre * sine).astype(BF16)

    flip = lax.axis_index("ent") * (n_rel * owner_rows)
    me_rel = lax.axis_index("rel")

    def row_id(i):
        at = i // owner_rows
        ent_bit = (at // (peers * n_rel)) | ((at // 2 % peers) << 1)
        rel_bit = at & 1
        for bit in range(n_rel.bit_length() - 2, 0, -1):
            rel_bit = rel_bit | (((at // (peers << bit)) & 1) << bit)
        return (ent_bit * n_rel + (rel_bit ^ me_rel)) * owner_rows + i % owner_rows

    e = row_id(lax.broadcasted_iota(I32, (entities, entities), 0))
    pick = jnp.where(e == lax.broadcasted_iota(I32, (entities, entities), 1), 1.0, 0.0).astype(BF16)
    wtf = lax.dot_general(pick, w_ref[...], NT, preferred_element_type=F32)
    counts = jnp.sum(wtf, axis=1, keepdims=True)
    heads = (owner_ref[...] * owner_rows + row_ref[...]) ^ flip
    eh = row_id(lax.broadcasted_iota(I32, (entities, n), 0))
    hot = jnp.where(eh == heads, 1.0, 0.0).astype(BF16)
    picked = jnp.dot(pick, tab, preferred_element_type=F32)
    cross = jnp.dot(wtf.astype(BF16), q_ref[...], preferred_element_type=F32)
    total = 2.0 * (cross - counts * picked) + jnp.dot(hot, hr[...], preferred_element_type=F32)
    keep_ref[...] = total[: entities // 2]
    send_ref[...] = total[entities // 2 :]


def scatter_kernel(mine_ref, theirs_ref, keep_ref, got_ref, *outs, shares, rows):
    chip = lax.axis_index("ent") // 2
    ids = jnp.concatenate([mine_ref[...], theirs_ref[...]], axis=1)
    d = jnp.concatenate([keep_ref[...], got_ref[...]], axis=0)
    n = ids.shape[1]
    iota = lax.broadcasted_iota(I32, (rows, n), 0)
    for out, (p, first) in zip(outs, shares):
        base = (chip ^ p) * (rows * (2 if p == 0 else 1)) + first
        hot = jnp.where(iota == ids - base, 1.0, 0.0).astype(BF16)
        out[...] = jnp.dot(hot, d, preferred_element_type=F32).astype(out.dtype)


def combine_kernel(low_ref, high_ref, *refs, peers, cols):
    got_refs, (left_ref, right_ref, keep_ref), outs = refs[: peers - 1], refs[peers - 1 : peers + 2], refs[peers + 2 :]
    total = jnp.concatenate([low_ref[...], high_ref[...]], axis=0)
    rows = total.shape[0]
    for got_ref in got_refs:
        total = total + got_ref[...].astype(F32)
    final = total.astype(BF16)
    ent = left_ref[...] + right_ref[...].astype(F32)
    span = ent.shape[0] // peers
    for p in range(peers):
        outs[p][:rows, :] = final
        chunk = ent[p * span : (p + 1) * span]
        if p == 0:
            keep_ref[...] = chunk
        else:
            blocks = [chunk[:, i : i + cols] for i in range(0, chunk.shape[1], cols)]
            outs[p][rows:, :] = jnp.concatenate(blocks, axis=0).astype(BF16)


def collect_kernel(keep_ref, *refs, rows, cols):
    got_refs, (mine_ref, other_ref) = refs[:-2], refs[-2:]
    span, width = keep_ref.shape
    total = keep_ref[...]
    for got_ref in got_refs:
        extra = got_ref[rows:, :].astype(F32)
        total = total + jnp.concatenate([extra[i * span : (i + 1) * span] for i in range(width // cols)], axis=1)
    mine_ref[...] = total[: span // 2]
    other_ref[...] = total[span // 2 :]


def place_kernel(src_ref, *refs, side, peers, rows):
    out_hbm, buf, sems = refs[-3:]
    quarter = src_ref.shape[1]
    me = lax.axis_index("ent")
    chip, par = me // 2, me % 2
    col = pl.multiple_of((par ^ side) * quarter, quarter)
    copies = []
    for p in range(peers):
        row = pl.multiple_of((chip ^ p) * rows, rows)
        at = slice(p * rows, (p + 1) * rows)
        buf[at, :] = src_ref[at, :].astype(F32)
        copies.append(pltpu.make_async_copy(buf.at[at, :], out_hbm.at[pl.ds(row, rows), pl.ds(col, quarter)], sems.at[p]))
        copies[-1].start()
    for copy in copies:
        copy.wait()


def local(entity_table, phases, head_owner, head_row, relation, tail_ids, known_tails):
    n_ent = lax.axis_size("ent")
    n_rel = lax.axis_size("rel")
    peers = n_ent // 2
    n = head_row.shape[0]
    rows_ent, width = entity_table.shape
    owner_rows = rows_ent // n_rel
    entities = rows_ent * n_ent
    half = width // 2
    quarter = half // 2
    rels = phases.shape[0]
    rows = rels // peers
    block = min(512, n)

    def swap(x, k):
        return lax.ppermute(x, "ent", [(i, i ^ k) for i in range(n_ent)])

    def swap_each(xs, order):
        got = dict(zip(order, lax.optimization_barrier([swap(xs[p], 2 * p) for p in order])))
        return [got[p] for p in range(1, peers)]

    def hold(x):
        return pltpu.with_memory_space_constraint(x, pltpu.HBM)

    middle = [peers // 2] if peers > 1 else []
    near = [p for p in range(1, peers // 2)]
    far = [p for p in range(peers // 2 + 1, peers)]
    ORD = {"yxd": middle + near + far, "ydx": middle + far + near, "xyd": near + middle + far, "dyx": far + middle + near, "dxy": far + near + middle}

    def swap_rel(x, k):
        return lax.ppermute(x, "rel", [(i, i ^ k) for i in range(n_rel)])

    hbm = pl.BlockSpec(memory_space=pltpu.HBM)
    vm = pl.BlockSpec(memory_space=pltpu.VMEM)

    owner_l = head_owner.reshape(1, n)
    row_l = head_row.reshape(1, n)
    rel_l = relation.reshape(1, n)
    tail_l = tail_ids.reshape(1, n)
    known_l = known_tails.T
    far = swap_each([entity_table] * peers, ORD["xyd"])
    fetched = [relation, phases, owner_l, row_l, tail_l, known_l, entity_table]
    cosine, sine, code, own = pl.pallas_call(
        functools.partial(prepare_kernel, rows_ent=rows_ent, owner_rows=owner_rows),
        in_specs=[hbm] * len(fetched),
        out_specs=[vm] * 4,
        out_shape=[
            jax.ShapeDtypeStruct((n, half), F32),
            jax.ShapeDtypeStruct((n, half), F32),
            jax.ShapeDtypeStruct((n, entities), I32),
            jax.ShapeDtypeStruct(entity_table.shape, BF16),
        ],
        scratch_shapes=[pltpu.SMEM((n,), I32)]
        + [pltpu.VMEM(x.shape, x.dtype) for x in fetched[1:6]]
        + [pltpu.SemaphoreType.DMA((len(fetched),))],
        compiler_params=params(),
        cost_estimate=cost(30 * n * half, 12 * n * half),
        name="prepare",
    )(*[hold(x) for x in fetched])

    cosine, sine, code, own, *far = lax.optimization_barrier((cosine, sine, code, own, *far))
    held = jnp.concatenate([own, *far], axis=0)
    mate, rel_mate = lax.optimization_barrier((swap(held, 1), swap(rel_l, 1)))
    tables = [held, mate]
    keep, send, w, q = pl.pallas_call(
        functools.partial(score_kernel, peers=peers, block=block),
        in_specs=[vm] * 5,
        out_specs=[vm] * 4,
        out_shape=[
            jax.ShapeDtypeStruct((n, quarter), BF16),
            jax.ShapeDtypeStruct((n, quarter), BF16),
            jax.ShapeDtypeStruct((n, entities), BF16),
            jax.ShapeDtypeStruct((n, width), BF16),
        ],
        compiler_params=params(),
        cost_estimate=cost(6 * n * entities * width, 12 * n * width),
        name="score",
    )(*tables, cosine, sine, code)

    got = swap(send, 1)
    ent_keep, ent_send = pl.pallas_call(
        functools.partial(entity_kernel, peers=peers, n_rel=n_rel, owner_rows=owner_rows, block=block),
        in_specs=[vm] * 8,
        out_specs=[vm] * 2,
        out_shape=[jax.ShapeDtypeStruct((entities // 2, width), F32)] * 2,
        scratch_shapes=[pltpu.VMEM((n, width), BF16)],
        compiler_params=params(),
        cost_estimate=cost(6 * n * entities * width, 4 * n * width + 4 * entities * width),
        name="entity",
    )(w, q, cosine, sine, owner_l, row_l, *tables)

    def scatter(shares, rows, dtype, work):
        return pl.pallas_call(
            functools.partial(scatter_kernel, shares=shares, rows=rows),
            in_specs=[vm] * 4,
            out_specs=[vm] * len(shares),
            out_shape=[jax.ShapeDtypeStruct((rows, quarter), dtype)] * len(shares),
            compiler_params=params(),
            cost_estimate=work,
            name="scatter",
        )(rel_l, rel_mate, keep, got)

    parts = scatter([(p, 0) for p in range(1, peers)], rows, BF16, cost(4 * n * rels * quarter, 4 * n * quarter + 2 * rels * quarter))
    *parts, ent_keep, ent_send = lax.optimization_barrier((*parts, ent_keep, ent_send))

    parts = [None, *parts]
    low, = scatter([(0, 0)], rows // 2, F32, cost(10**9, 8 * n * quarter))
    high, = scatter([(0, rows // 2)], rows // 2, F32, cost(10**9, 8 * n * quarter))
    received = swap_each(parts, ORD["xyd"])

    left, right = ent_keep, swap(ent_send, 1)
    for bit in range(n_rel.bit_length() - 2, 0, -1):
        middle = left.shape[0] // 2
        left, right = (left + right)[:middle], swap_rel((left + right)[middle:].astype(BF16), 1 << bit)
    span = 2 * owner_rows
    extra = span * width // quarter
    ent_own, *messages = pl.pallas_call(
        functools.partial(combine_kernel, peers=peers, cols=quarter),
        in_specs=[vm] * (peers + 3),
        out_specs=[vm] * (peers + 1),
        out_shape=[jax.ShapeDtypeStruct((span, width), F32), jax.ShapeDtypeStruct((rows, quarter), BF16)]
        + [jax.ShapeDtypeStruct((rows + extra, quarter), BF16)] * (peers - 1),
        compiler_params=params(),
        cost_estimate=cost(4 * rows * quarter, 16 * rows * quarter),
        name="combine",
    )(low, high, *received, left, right)
    final, far = messages[0], swap_each(messages, ORD["dxy"])
    mine = jnp.concatenate([final] + [x[:rows] for x in far], axis=0)
    left, right = pl.pallas_call(
        functools.partial(collect_kernel, rows=rows, cols=quarter),
        in_specs=[vm] * peers,
        out_specs=[vm] * 2,
        out_shape=[jax.ShapeDtypeStruct((owner_rows, width), F32)] * 2,
        compiler_params=params(),
        cost_estimate=cost(peers * span * width, 4 * peers * span * width),
        name="collect",
    )(ent_own, *far)
    theirs = swap(mine, 1)
    right = swap_rel(right, 1)

    gradient = jax.ShapeDtypeStruct((rels, half), F32)

    def place(side, *args):
        return pl.pallas_call(
            functools.partial(place_kernel, side=side, peers=peers, rows=rows),
            in_specs=[vm, hbm][: len(args)],
            out_specs=hbm,
            out_shape=gradient,
            scratch_shapes=[pltpu.VMEM((rels, quarter), F32), pltpu.SemaphoreType.DMA((peers,))],
            input_output_aliases={1: 0} if side else {},
            compiler_params=params(),
            cost_estimate=cost(rels * half, 6 * rels * half),
            name="place",
        )(*args)

    relation_gradient = place(1, theirs, place(0, mine))
    relation_gradient, left, right = lax.optimization_barrier((relation_gradient, left, right))
    return left + right, relation_gradient


def solution(mesh):
    in_specs = (
        P("ent", None),
        P("rel", None),
        P(("ent", "rel"), None),
        P(("ent", "rel")),
        P(("ent", "rel")),
        P(("ent", "rel")),
        P(("ent", "rel"), None),
    )
    out_specs = (P(("ent", "rel"), None), P("rel", None))
    return jax.shard_map(local, mesh=mesh, in_specs=in_specs, out_specs=out_specs, check_vma=False)
```

```python
import functools

import jax
import jax.numpy as jnp
from jax import lax
from jax.experimental import pallas as pl
from jax.experimental.pallas import tpu as pltpu
from jax.sharding import PartitionSpec as P

F32 = jnp.float32
BF16 = jnp.bfloat16
I32 = jnp.int32
DIGIT = 64
VMEM_BYTES = 16 * 1024 * 1024
NT = (((1,), (1,)), ((), ()))

SIN_C = (0.9999999957, -0.1666665799, 0.008333051133, -0.0001980908535, 2.605256611e-06)
COS_C = (0.9999999998, -0.4999999936, 0.04166663628, -0.00138883618, 2.476018568e-05, -2.605198025e-07)


def params():
    return pltpu.CompilerParams(vmem_limit_bytes=VMEM_BYTES)


def cost(flops, nbytes, trans=0):
    return pl.CostEstimate(flops=flops, bytes_accessed=nbytes, transcendentals=trans)


def horner(coeffs, y):
    acc = jnp.full_like(y, coeffs[-1])
    for c in coeffs[-2::-1]:
        acc = acc * y + c
    return acc


def prepare_kernel(
    rel_hbm, phases_hbm, owner_hbm, row_hbm, tail_hbm, known_hbm, table_hbm, cos_ref, sin_ref, code_ref, own_ref,
    rel_ref, phases_ref, owner_ref, row_ref, tail_ref, known_ref, sems, *, rows_ent, owner_rows,
):
    n = cos_ref.shape[0]
    pairs = [(known_hbm, known_ref), (owner_hbm, owner_ref), (row_hbm, row_ref), (tail_hbm, tail_ref)]
    pairs += [(rel_hbm, rel_ref), (phases_hbm, phases_ref), (table_hbm, own_ref)]
    copies = [pltpu.make_async_copy(src, dst, sems.at[i]) for i, (src, dst) in enumerate(pairs)]
    for copy in copies:
        copy.start()
    for copy in copies[:4]:
        copy.wait()
    flip = lax.axis_index("ent") * rows_ent
    entities = code_ref.shape[1]
    lanes = min(128, n)
    sub = lax.broadcasted_iota(I32, (8, lanes), 0)
    for start in range(0, n, lanes):
        at = slice(start, start + lanes)
        heads = (owner_ref[:, at] * owner_rows + row_ref[:, at]) ^ flip
        tails = tail_ref[:, at] ^ flip
        known = known_ref[:, at] ^ flip
        bits = lax.shift_left(jnp.ones_like(known), known & 31)
        word_of = lax.shift_right_logical(known, 5)
        pieces = []
        for w in range(entities // 32):
            hit = jnp.where(word_of == w, bits, 0)
            word = hit[0:8]
            for r in range(8, hit.shape[0], 8):
                word = word | hit[r : r + 8]
            for shift in (4, 2, 1):
                word = word | pltpu.roll(word, shift, 0)
            for g in range(4):
                e = sub + (32 * w + 8 * g)
                listed = lax.shift_right_logical(word, sub + 8 * g) & 1
                target = jnp.where(e == tails, 1, 0)
                head = jnp.where(e == heads, 4, 0)
                pieces.append((listed & (1 - target)) | (target * 2) | head)
        code_ref[at, :] = jnp.concatenate(pieces, axis=0).T

    for copy in copies[4:]:
        copy.wait()
    half = cos_ref.shape[1]
    place = lax.broadcasted_iota(I32, (8, half), 0)
    for start in range(0, n, 8):
        angle = jnp.broadcast_to(phases_ref[pl.ds(rel_ref[start], 1), :], (8, half))
        for j in range(1, 8):
            angle = jnp.where(place == j, jnp.broadcast_to(phases_ref[pl.ds(rel_ref[start + j], 1), :], (8, half)), angle)
        u = angle * 0.5
        y = u * u
        s = u * horner(SIN_C, y)
        t = 2.0 * s
        sin_ref[start : start + 8, :] = t * horner(COS_C, y)
        cos_ref[start : start + 8, :] = 1.0 - t * s


def candidates(own_ref, mate_ref, peers):
    step = own_ref.shape[0] // peers
    blocks = [ref[p * step : (p + 1) * step, :] for p in range(peers) for ref in (own_ref, mate_ref)]
    return jnp.concatenate(blocks, axis=0)


def score_kernel(*refs, peers, block):
    own_ref, mate_ref, rel_ref, cos_ref, sin_ref, code_ref, keep_ref, send_ref, w_ref, q_ref = refs
    n, half = cos_ref.shape
    quarter = half // 2
    tab = candidates(own_ref, mate_ref, peers)
    f = tab.astype(F32)
    norm = jnp.sum(f * f, axis=1, keepdims=True)
    tsq = jnp.broadcast_to(norm, (norm.shape[0], 128)).T[0:1]
    even = lax.axis_index("ent") % 2 == 0
    rel = rel_ref[...].astype(F32)
    high = jnp.floor(rel * (1.0 / DIGIT))
    lines = [x[:, i : i + quarter] for x in (high, rel - DIGIT * high) for i in range(0, n, quarter)]
    lines.append(jnp.zeros((send_ref.shape[0] - n - len(lines), quarter), F32))
    send_ref[n:, :] = jnp.concatenate(lines, axis=0).astype(BF16)
    for start in range(0, n, block):
        at = slice(start, start + block)
        cosine = cos_ref[at, :]
        sine = sin_ref[at, :]
        code = code_ref[at, :]
        hot = jnp.where((code & 4) != 0, 1.0, 0.0).astype(BF16)
        head = jnp.dot(hot, tab, preferred_element_type=F32)
        hre = head[:, :half]
        him = head[:, half:]
        qre = hre * cosine - him * sine
        qim = hre * sine + him * cosine
        q = jnp.concatenate([qre, qim], axis=1).astype(BF16)
        q_ref[at, :] = q
        qf = q.astype(F32)
        qsq = jnp.sum(qf * qf, axis=1, keepdims=True)
        cross = lax.dot_general(q, tab, NT, preferred_element_type=F32)
        scores = 2.0 * cross - qsq - tsq
        masked = (code & 1) != 0
        target = jnp.where((code & 2) != 0, 1.0, 0.0)
        row_max = jnp.max(jnp.where(masked, -jnp.inf, scores), axis=1, keepdims=True)
        raw = jnp.where(masked, 0.0, jnp.exp(scores - row_max))
        prob = raw / jnp.sum(raw, axis=1, keepdims=True)
        w = (prob - target).astype(BF16)
        w_ref[at, :] = w
        dq = jnp.dot(w + w, tab, preferred_element_type=F32)
        dangle = (qre * dq[:, half:] - qim * dq[:, :half]).astype(BF16)
        first = dangle[:, :quarter]
        second = dangle[:, quarter:]
        keep_ref[at, :] = jnp.where(even, first, second)
        send_ref[at, :] = jnp.where(even, second, first)


def entity_kernel(w_ref, q_ref, cos_ref, sin_ref, owner_ref, row_ref, *refs, peers, n_rel, owner_rows, block):
    own_ref, mate_ref, keep_ref, send_ref, hr = refs
    n, entities = w_ref.shape
    half = cos_ref.shape[1]
    tab = candidates(own_ref, mate_ref, peers)
    for start in range(0, n, block):
        at = slice(start, start + block)
        w = w_ref[at, :]
        dq = jnp.dot(w + w, tab, preferred_element_type=F32)
        cosine = cos_ref[at, :]
        sine = sin_ref[at, :]
        dre = dq[:, :half]
        dim = dq[:, half:]
        hr[at, :half] = (dre * cosine + dim * sine).astype(BF16)
        hr[at, half:] = (dim * cosine - dre * sine).astype(BF16)

    flip = lax.axis_index("ent") * (n_rel * owner_rows)
    me_rel = lax.axis_index("rel")

    def row_id(i):
        at = i // owner_rows
        ent_bit = (at // (peers * n_rel)) | ((at // 2 % peers) << 1)
        rel_bit = at & 1
        for bit in range(n_rel.bit_length() - 2, 0, -1):
            rel_bit = rel_bit | (((at // (peers << bit)) & 1) << bit)
        return (ent_bit * n_rel + (rel_bit ^ me_rel)) * owner_rows + i % owner_rows

    e = row_id(lax.broadcasted_iota(I32, (entities, entities), 0))
    pick = jnp.where(e == lax.broadcasted_iota(I32, (entities, entities), 1), 1.0, 0.0).astype(BF16)
    wtf = lax.dot_general(pick, w_ref[...], NT, preferred_element_type=F32)
    counts = jnp.sum(wtf, axis=1, keepdims=True)
    heads = (owner_ref[...] * owner_rows + row_ref[...]) ^ flip
    eh = row_id(lax.broadcasted_iota(I32, (entities, n), 0))
    hot = jnp.where(eh == heads, 1.0, 0.0).astype(BF16)
    picked = jnp.dot(pick, tab, preferred_element_type=F32)
    cross = jnp.dot(wtf.astype(BF16), q_ref[...], preferred_element_type=F32)
    total = 2.0 * (cross - counts * picked) + jnp.dot(hot, hr[...], preferred_element_type=F32)
    keep_ref[...] = total[: entities // 2]
    send_ref[...] = total[entities // 2 :]


def scatter_kernel(mine_ref, keep_ref, got_ref, *outs, shares, rows):
    chip = lax.axis_index("ent") // 2
    count, quarter = keep_ref.shape
    lines = count // quarter
    digits = got_ref[count:, :].astype(F32)
    theirs = [digits[i : i + 1] * DIGIT + digits[lines + i : lines + i + 1] for i in range(lines)]
    ids = jnp.concatenate([mine_ref[...]] + [x.astype(I32) for x in theirs], axis=1)
    d = jnp.concatenate([keep_ref[...], got_ref[:count, :]], axis=0)
    n = ids.shape[1]
    iota = lax.broadcasted_iota(I32, (rows, n), 0)
    for out, (p, first) in zip(outs, shares):
        base = (chip ^ p) * (rows * (2 if p == 0 else 1)) + first
        hot = jnp.where(iota == ids - base, 1.0, 0.0).astype(BF16)
        out[...] = jnp.dot(hot, d, preferred_element_type=F32).astype(out.dtype)


def combine_kernel(low_ref, high_ref, *refs, peers, cols):
    got_refs, (left_ref, right_ref, keep_ref), outs = refs[: peers - 1], refs[peers - 1 : peers + 2], refs[peers + 2 :]
    total = jnp.concatenate([low_ref[...], high_ref[...]], axis=0)
    rows = total.shape[0]
    for got_ref in got_refs:
        total = total + got_ref[...].astype(F32)
    final = total.astype(BF16)
    ent = left_ref[...] + right_ref[...].astype(F32)
    span = ent.shape[0] // peers
    for p in range(peers):
        outs[p][:rows, :] = final
        chunk = ent[p * span : (p + 1) * span]
        if p == 0:
            keep_ref[...] = chunk
        else:
            blocks = [chunk[:, i : i + cols] for i in range(0, chunk.shape[1], cols)]
            outs[p][rows:, :] = jnp.concatenate(blocks, axis=0).astype(BF16)


def collect_kernel(keep_ref, *refs, rows, cols):
    got_refs, (mine_ref, other_ref) = refs[:-2], refs[-2:]
    span, width = keep_ref.shape
    total = keep_ref[...]
    for got_ref in got_refs:
        extra = got_ref[rows:, :].astype(F32)
        total = total + jnp.concatenate([extra[i * span : (i + 1) * span] for i in range(width // cols)], axis=1)
    mine_ref[...] = total[: span // 2]
    other_ref[...] = total[span // 2 :]


def place_kernel(src_ref, *refs, side, peers, rows):
    out_hbm, buf, sems = refs[-3:]
    quarter = src_ref.shape[1]
    me = lax.axis_index("ent")
    chip, par = me // 2, me % 2
    col = pl.multiple_of((par ^ side) * quarter, quarter)
    copies = []
    for p in range(peers):
        row = pl.multiple_of((chip ^ p) * rows, rows)
        at = slice(p * rows, (p + 1) * rows)
        buf[at, :] = src_ref[at, :].astype(F32)
        copies.append(pltpu.make_async_copy(buf.at[at, :], out_hbm.at[pl.ds(row, rows), pl.ds(col, quarter)], sems.at[p]))
        copies[-1].start()
    for copy in copies:
        copy.wait()


def local(entity_table, phases, head_owner, head_row, relation, tail_ids, known_tails):
    n_ent = lax.axis_size("ent")
    n_rel = lax.axis_size("rel")
    peers = n_ent // 2
    n = head_row.shape[0]
    rows_ent, width = entity_table.shape
    owner_rows = rows_ent // n_rel
    entities = rows_ent * n_ent
    half = width // 2
    quarter = half // 2
    rels = phases.shape[0]
    rows = rels // peers
    block = min(512, n)

    def swap(x, k):
        return lax.ppermute(x, "ent", [(i, i ^ k) for i in range(n_ent)])

    def swap_each(xs, order):
        got = dict(zip(order, lax.optimization_barrier([swap(xs[p], 2 * p) for p in order])))
        return [got[p] for p in range(1, peers)]

    def hold(x):
        return pltpu.with_memory_space_constraint(x, pltpu.HBM)

    middle = [peers // 2] if peers > 1 else []
    near = [p for p in range(1, peers // 2)]
    far = [p for p in range(peers // 2 + 1, peers)]
    ORD = {"yxd": middle + near + far, "ydx": middle + far + near, "xyd": near + middle + far, "dyx": far + middle + near, "dxy": far + near + middle}

    def swap_rel(x, k):
        return lax.ppermute(x, "rel", [(i, i ^ k) for i in range(n_rel)])

    hbm = pl.BlockSpec(memory_space=pltpu.HBM)
    vm = pl.BlockSpec(memory_space=pltpu.VMEM)

    owner_l = head_owner.reshape(1, n)
    row_l = head_row.reshape(1, n)
    rel_l = relation.reshape(1, n)
    tail_l = tail_ids.reshape(1, n)
    known_l = known_tails.T
    far = swap_each([entity_table] * peers, ORD["xyd"])
    fetched = [relation, phases, owner_l, row_l, tail_l, known_l, entity_table]
    cosine, sine, code, own = pl.pallas_call(
        functools.partial(prepare_kernel, rows_ent=rows_ent, owner_rows=owner_rows),
        in_specs=[hbm] * len(fetched),
        out_specs=[vm] * 4,
        out_shape=[
            jax.ShapeDtypeStruct((n, half), F32),
            jax.ShapeDtypeStruct((n, half), F32),
            jax.ShapeDtypeStruct((n, entities), I32),
            jax.ShapeDtypeStruct(entity_table.shape, BF16),
        ],
        scratch_shapes=[pltpu.SMEM((n,), I32)]
        + [pltpu.VMEM(x.shape, x.dtype) for x in fetched[1:6]]
        + [pltpu.SemaphoreType.DMA((len(fetched),))],
        compiler_params=params(),
        cost_estimate=cost(30 * n * half, 12 * n * half),
        name="prepare",
    )(*[hold(x) for x in fetched])

    cosine, sine, code, own, *far = lax.optimization_barrier((cosine, sine, code, own, *far))
    held = jnp.concatenate([own, *far], axis=0)
    tables = [held, swap(held, 1)]
    digit_rows = -(-2 * (n // quarter) // 16) * 16
    keep, send, w, q = pl.pallas_call(
        functools.partial(score_kernel, peers=peers, block=block),
        in_specs=[vm] * 6,
        out_specs=[vm] * 4,
        out_shape=[
            jax.ShapeDtypeStruct((n, quarter), BF16),
            jax.ShapeDtypeStruct((n + digit_rows, quarter), BF16),
            jax.ShapeDtypeStruct((n, entities), BF16),
            jax.ShapeDtypeStruct((n, width), BF16),
        ],
        compiler_params=params(),
        cost_estimate=cost(6 * n * entities * width, 12 * n * width),
        name="score",
    )(*tables, rel_l, cosine, sine, code)

    got = swap(send, 1)
    ent_keep, ent_send = pl.pallas_call(
        functools.partial(entity_kernel, peers=peers, n_rel=n_rel, owner_rows=owner_rows, block=block),
        in_specs=[vm] * 8,
        out_specs=[vm] * 2,
        out_shape=[jax.ShapeDtypeStruct((entities // 2, width), F32)] * 2,
        scratch_shapes=[pltpu.VMEM((n, width), BF16)],
        compiler_params=params(),
        cost_estimate=cost(6 * n * entities * width, 4 * n * width + 4 * entities * width),
        name="entity",
    )(w, q, cosine, sine, owner_l, row_l, *tables)

    def scatter(shares, rows, dtype, work):
        return pl.pallas_call(
            functools.partial(scatter_kernel, shares=shares, rows=rows),
            in_specs=[vm] * 3,
            out_specs=[vm] * len(shares),
            out_shape=[jax.ShapeDtypeStruct((rows, quarter), dtype)] * len(shares),
            compiler_params=params(),
            cost_estimate=work,
            name="scatter",
        )(rel_l, keep, got)

    parts = scatter([(p, 0) for p in range(1, peers)], rows, BF16, cost(4 * n * rels * quarter, 4 * n * quarter + 2 * rels * quarter))
    *parts, ent_keep, ent_send = lax.optimization_barrier((*parts, ent_keep, ent_send))

    parts = [None, *parts]
    low, = scatter([(0, 0)], rows // 2, F32, cost(10**9, 8 * n * quarter))
    high, = scatter([(0, rows // 2)], rows // 2, F32, cost(10**9, 8 * n * quarter))
    received = swap_each(parts, ORD["xyd"])

    left, right = ent_keep, swap(ent_send, 1)
    for bit in range(n_rel.bit_length() - 2, 0, -1):
        middle = left.shape[0] // 2
        left, right = (left + right)[:middle], swap_rel((left + right)[middle:].astype(BF16), 1 << bit)
    span = 2 * owner_rows
    extra = span * width // quarter
    ent_own, *messages = pl.pallas_call(
        functools.partial(combine_kernel, peers=peers, cols=quarter),
        in_specs=[vm] * (peers + 3),
        out_specs=[vm] * (peers + 1),
        out_shape=[jax.ShapeDtypeStruct((span, width), F32), jax.ShapeDtypeStruct((rows, quarter), BF16)]
        + [jax.ShapeDtypeStruct((rows + extra, quarter), BF16)] * (peers - 1),
        compiler_params=params(),
        cost_estimate=cost(4 * rows * quarter, 16 * rows * quarter),
        name="combine",
    )(low, high, *received, left, right)
    final, far = messages[0], swap_each(messages, ORD["dxy"])
    mine = jnp.concatenate([final] + [x[:rows] for x in far], axis=0)
    left, right = pl.pallas_call(
        functools.partial(collect_kernel, rows=rows, cols=quarter),
        in_specs=[vm] * peers,
        out_specs=[vm] * 2,
        out_shape=[jax.ShapeDtypeStruct((owner_rows, width), F32)] * 2,
        compiler_params=params(),
        cost_estimate=cost(peers * span * width, 4 * peers * span * width),
        name="collect",
    )(ent_own, *far)
    theirs = swap(mine, 1)
    right = swap_rel(right, 1)

    gradient = jax.ShapeDtypeStruct((rels, half), F32)

    def place(side, *args):
        return pl.pallas_call(
            functools.partial(place_kernel, side=side, peers=peers, rows=rows),
            in_specs=[vm, hbm][: len(args)],
            out_specs=hbm,
            out_shape=gradient,
            scratch_shapes=[pltpu.VMEM((rels, quarter), F32), pltpu.SemaphoreType.DMA((peers,))],
            input_output_aliases={1: 0} if side else {},
            compiler_params=params(),
            cost_estimate=cost(rels * half, 6 * rels * half),
            name="place",
        )(*args)

    relation_gradient = place(1, theirs, place(0, mine))
    relation_gradient, left, right = lax.optimization_barrier((relation_gradient, left, right))
    return left + right, relation_gradient


def solution(mesh):
    in_specs = (
        P("ent", None),
        P("rel", None),
        P(("ent", "rel"), None),
        P(("ent", "rel")),
        P(("ent", "rel")),
        P(("ent", "rel")),
        P(("ent", "rel"), None),
    )
    out_specs = (P(("ent", "rel"), None), P("rel", None))
    return jax.shard_map(local, mesh=mesh, in_specs=in_specs, out_specs=out_specs, check_vma=False)
```
